32 devices in a mesh: scan: 2 (over x), tile: 16 (over z, y, core).
Axes of the slice: x: 2, y: 2, z: 4, core: 2. Of those that a mesh axis runs over, the one named last changes fastest.
Arguments:
- coefficients: bfloat16 [66, 2048], P(None, 'tile'), may hold values from -0.75 to 0.75
- zernike_table: bfloat16 [66, 4096], replicated, may hold values from -6 to 6
- positions: int32 [32, 256], P('scan'), parts along dimension 0, may hold values from 0 to 4095
- source_flux: float32 [32, 256], P('scan'), parts along dimension 0, may hold values from 0.5 to 2
- observed: bfloat16 [2112, 16, 4096], P(('scan', 'tile')), parts along dimension 0, may hold values from -6 to 6
- tile_rows: int32 [2112], P(('scan', 'tile')), parts along dimension 0, may hold values from 0 to 31, as said below
- tile_cols: int32 [2112], P(('scan', 'tile')), parts along dimension 0, may hold values from 0 to 31, as said below
- tile_count: int32 [32], P(('scan', 'tile')), parts along dimension 0, may hold values from 0 to 66, as said below
Outputs:
- coeff_grad: float32 [132, 2048], P('scan', 'tile'), parts along dimension 0
The draws below stay inside these ranges and needn't reach their ends.
There are 2 independent parts, one for each index of `scan`. The reference program is written for one: setup_inputs(seed, part) draws one part's arguments, and reference() takes and returns one part's arrays. A program takes and returns all parts, laid end to end along the dimension named above; an argument that names none is the same for every part. Nothing has to cross between parts.
Inputs may be any that keep to these rules, and one draw needn't show every extreme that they name: `tile_rows`: the live slots of a part hold every pair of dish blocks with row block at most column block exactly once; slots that are not live hold 0. `tile_cols`: column block of the same slot as tile_rows; never below its row block in a live slot. `tile_count`: live slots come first on each device; one device of every part has exactly 66 live slots.
All inputs are finite; a program needn't handle non-finite values.
Results may differ from the reference program's by a relative error of at most 0.0012.
Values may be sent and summed in bfloat16 or wider, within the bound.
No kernel may reach another device: no remote copies, remote signals or barrier semaphores. Data moves between devices by JAX's collectives and lax.ppermute only.
A program may use at most 128 MiB of HBM per device.

```python
import math
import jax
import jax.numpy as jnp
import numpy as np
from jax import lax

DISHES = 2048
K = 66
BLK = 64
PIX = 4096
F = 16
S = 256
NBLK = 32
TILES = 528
SLOTS = 66
MEMBERS = 16
SLOT_ROWS = 1056


def assignment(key):
    row_all, col_all = np.triu_indices(NBLK)
    first_key, second_key = jax.random.split(key)
    order = jax.random.permutation(first_key, TILES)
    devices = jax.random.permutation(second_key, MEMBERS)
    position = jnp.arange(TILES, dtype=jnp.int32)
    remainder = jnp.maximum(position - SLOTS, 0)
    on_heavy = position < SLOTS
    device = jnp.where(on_heavy, devices[0], devices[1 + remainder % (MEMBERS - 1)])
    slot_index = jnp.where(on_heavy, position, remainder // (MEMBERS - 1))
    flat_index = device * SLOTS + slot_index
    row_flat = jnp.zeros((MEMBERS * SLOTS,), jnp.int32).at[flat_index].set(jnp.asarray(row_all, jnp.int32)[order])
    col_flat = jnp.zeros((MEMBERS * SLOTS,), jnp.int32).at[flat_index].set(jnp.asarray(col_all, jnp.int32)[order])
    counts = jnp.zeros((MEMBERS,), jnp.int32).at[device].add(1)
    return (row_flat, col_flat, counts)


def draw_tile_rows(key, part):
    row_flat, col_flat, counts = assignment(key)
    return row_flat


def draw_tile_cols(key, part):
    row_flat, col_flat, counts = assignment(key)
    return col_flat


def draw_tile_count(key, part):
    row_flat, col_flat, counts = assignment(key)
    return counts


def plant(result, own_key, least, largest):
    longest = result.shape.index(max(result.shape))
    spots = []
    for shift in (0, 1):
        where = [jax.random.randint(jax.random.fold_in(own_key, axis), (), 0, length) for axis, length in enumerate(result.shape)]
        where[longest] = (where[longest] + shift) % result.shape[longest]
        spots.append(tuple(where))
    return result.at[spots[0]].set(least).at[spots[1]].set(largest)


def steps_of(stream_key, extent, pieces, low, largest):
    factor_of = 1.0
    for dim, parts in pieces:
        heights = jax.random.uniform(jax.random.fold_in(jax.random.fold_in(stream_key, 6), dim), (parts,), jnp.float32, low / len(pieces), largest / len(pieces))
        factor_of = factor_of * jnp.repeat(jnp.exp(heights), extent[dim] // parts).reshape((-1,) + (1,) * (len(extent) - 1 - dim))
    return factor_of


def noise(rng, extent, width, reach, shards=(), held_as=jnp.bfloat16):
    level = steps_of(rng, extent, shards, -0.22, 0.18) if shards else 1.0
    values = jax.random.normal(rng, extent, jnp.float32) * width * level
    return jnp.minimum(jnp.maximum(values, -reach), reach).astype(held_as)


def setup_inputs(seed: int = 0, part: int = 0) -> dict:
    key_of = jax.random.split(jax.random.key(seed), 9)
    part_splits = jax.random.split(jax.random.fold_in(key_of[8], part), 9)
    return {
        "coefficients": noise(key_of[0], (K, DISHES), K ** -0.5, 0.75, ((1, 16),)),
        "zernike_table": noise(key_of[1], (K, PIX), 1.0, 6.0),
        "positions": plant(jax.random.randint(part_splits[2], (F, S), 0, PIX), jax.random.fold_in(part_splits[2], 1), 0, PIX - 1).astype(jnp.int32),
        "source_flux": jnp.clip(jnp.exp(jax.random.uniform(part_splits[3], (F, S), jnp.float32, math.log(0.5), math.log(2.0))), 0.5, 2.0),
        "observed": noise(part_splits[4], (SLOT_ROWS, F, BLK * BLK), 1.0, 6.0, ((0, 16),)),
        "tile_rows": draw_tile_rows(jax.random.fold_in(jax.random.fold_in(key_of[8], part), 71), part),
        "tile_cols": draw_tile_cols(jax.random.fold_in(jax.random.fold_in(key_of[8], part), 71), part),
        "tile_count": draw_tile_count(jax.random.fold_in(jax.random.fold_in(key_of[8], part), 71), part),
    }


def reference(coefficients, zernike_table, positions, source_flux, observed, tile_rows, tile_cols, tile_count):
    selected = zernike_table[:, positions]
    beams = jnp.einsum('kp,kfs->fps', coefficients.astype(jnp.float32), selected.astype(jnp.float32)).astype(jnp.bfloat16)
    root = math.sqrt(S)
    weighted = (source_flux[:, None, :] * beams.astype(jnp.float32) / root).astype(jnp.bfloat16)
    slot_ids = jnp.arange(SLOT_ROWS, dtype=jnp.int32)
    live_slot = slot_ids % SLOTS < tile_count[slot_ids // SLOTS]
    target = jnp.where(live_slot, tile_rows * NBLK + tile_cols, NBLK * NBLK)
    pair_slot = jnp.zeros((NBLK * NBLK,), jnp.int32).at[target].set(slot_ids, mode='drop')
    upper_rows, upper_cols = np.triu_indices(NBLK)
    upper_rows = jnp.asarray(upper_rows, jnp.int32)
    upper_cols = jnp.asarray(upper_cols, jnp.int32)
    row_index = jnp.arange(BLK, dtype=jnp.int32)[:, None]
    col_index = jnp.arange(BLK, dtype=jnp.int32)[None, :]
    zero = jnp.zeros((), jnp.int32)

    def add_tile(total, pair):
        left_block, right_block = pair
        slot = pair_slot[left_block * NBLK + right_block]
        piece = observed[slot].reshape(F, BLK, BLK).astype(jnp.float32)
        left_start = left_block * BLK
        right_start = right_block * BLK
        left_weighted = lax.dynamic_slice(weighted, (zero, left_start, zero), (F, BLK, S))
        right_weighted = lax.dynamic_slice(weighted, (zero, right_start, zero), (F, BLK, S))
        right_beams = lax.dynamic_slice(beams, (zero, right_start, zero), (F, BLK, S))
        model = jnp.einsum('fis,fjs->fij', left_weighted.astype(jnp.float32), right_beams.astype(jnp.float32))
        keep = jnp.logical_or(left_block != right_block, col_index > row_index).astype(jnp.float32)
        residual = ((model - piece) * keep).astype(jnp.bfloat16).astype(jnp.float32)
        row_grad = jnp.einsum('fij,fjs->fis', residual, right_weighted.astype(jnp.float32)).astype(jnp.bfloat16)
        col_grad = jnp.einsum('fij,fis->fjs', residual, left_weighted.astype(jnp.float32)).astype(jnp.bfloat16)
        current = lax.dynamic_slice(total, (zero, left_start, zero), (F, BLK, S))
        total = lax.dynamic_update_slice(total, current + row_grad.astype(jnp.float32), (zero, left_start, zero))
        current = lax.dynamic_slice(total, (zero, right_start, zero), (F, BLK, S))
        total = lax.dynamic_update_slice(total, current + col_grad.astype(jnp.float32), (zero, right_start, zero))
        return (total, None)
    start_total = jnp.zeros((F, DISHES, S), jnp.float32)
    beam_grad, unused = lax.scan(add_tile, start_total, (upper_rows, upper_cols))
    summed = jnp.einsum('fps,kfs->kp', beam_grad, selected.astype(jnp.float32), precision=lax.Precision.HIGHEST)
    return summed / math.sqrt(DISHES * F)
```

```python
import functools
import math

import jax
import jax.numpy as jnp
from jax import lax
from jax.experimental import pallas as pl
from jax.experimental.pallas import tpu as pltpu
from jax.sharding import PartitionSpec as P

BLK = 64
LANES = 128
PIXELS = 256
BF = jnp.bfloat16
F32 = jnp.float32
NT = (((1,), (1,)), ((), ()))


def up(size, unit):
    return -(-size // unit) * unit


def low_lanes(rows):
    return lax.broadcasted_iota(jnp.int32, (rows, LANES), 1) < BLK


def gram_kernel(root, table_ref, pos_ref, flux_ref, out_ref, groups, gram):
    terms, pixels = table_ref.shape
    channels, sources = pos_ref.shape
    n_groups = pixels // PIXELS
    tall = groups.shape[0] // n_groups
    rows = up(terms, 8)
    groups[...] = jnp.zeros_like(groups)
    gram[...] = jnp.zeros_like(gram)
    for h in range(n_groups):
        groups[h * tall : h * tall + terms, :] = table_ref[:, h * PIXELS : (h + 1) * PIXELS]
    pixel = lax.broadcasted_iota(jnp.int32, (PIXELS, sources), 0)
    for f in range(channels):
        pos = pos_ref[f : f + 1, :]
        hot = jnp.where(pixel == pos % PIXELS, 1.0, 0.0).astype(BF)
        found = jnp.dot(groups[...], hot, preferred_element_type=F32)
        group = pos // PIXELS
        chosen = jnp.zeros((tall, sources), F32)
        for h in range(n_groups):
            chosen = jnp.where(group == h, found[h * tall : (h + 1) * tall], chosen)
        scaled = chosen * (flux_ref[f : f + 1, :] / root)
        high = scaled.astype(BF)
        low = (scaled - high.astype(F32)).astype(BF)
        chosen = chosen.astype(BF)
        product = lax.dot_general(high, chosen, NT, preferred_element_type=F32)
        product = product + lax.dot_general(low, chosen, NT, preferred_element_type=F32)
        gram[f * rows : f * rows + tall, 0:tall] = product
    value = gram[...]
    high = value.astype(BF)
    out_ref[:, 0:LANES] = high
    out_ref[:, LANES : 2 * LANES] = (value - high.astype(F32)).astype(BF)


def gram_of(zernike_table, positions, source_flux):
    terms, pixels = zernike_table.shape
    channels, sources = positions.shape
    rows, tall = up(terms, 8), up(terms, 16)
    height = up(channels * rows + 8, 16)
    return pl.pallas_call(
        functools.partial(gram_kernel, math.sqrt(sources)),
        out_shape=jax.ShapeDtypeStruct((height, 2 * LANES), BF),
        in_specs=[pl.BlockSpec(memory_space=pltpu.VMEM)] * 3,
        out_specs=pl.BlockSpec(memory_space=pltpu.VMEM),
        scratch_shapes=[
            pltpu.VMEM((pixels // PIXELS * tall, PIXELS), BF),
            pltpu.VMEM((height, LANES), F32),
        ],
        compiler_params=pltpu.CompilerParams(vmem_limit_bytes=32 << 20),
        cost_estimate=pl.CostEstimate(
            flops=2 * channels * sources * pixels * terms, bytes_accessed=1 << 20, transcendentals=0
        ),
    )(zernike_table, positions, source_flux)


def reverse_bits(value, bits):
    result = value & 0
    for bit in range(bits):
        result = result | ((value >> bit) & 1) << (bits - 1 - bit)
    return result


def tiles_kernel(
    relative_bits, unroll, scale,
    count_ref, rows_ref, cols_ref, own_ref, got_ref, gram_ref, vis_hbm,
    keep_ref, send_ref,
    vis, stage, spread, plain, mixed, turned, right, left, row_sum, col_sum, sems,
):
    slots, channels = vis.shape[0], vis.shape[1]
    half, terms = own_ref.shape[0], own_ref.shape[1]
    pairs = channels // 2
    rows, tall = up(terms, 8), up(terms, 16)
    count = count_ref[0]
    n_groups = (count + unroll - 1) // unroll

    def fetch(slot):
        return pltpu.make_async_copy(vis_hbm.at[slot], vis.at[slot], sems.at[slot])

    @pl.loop(0, n_groups * unroll)
    def _(slot):
        fetch(slot).start()

    row_sum[...] = jnp.zeros_like(row_sum)
    col_sum[...] = jnp.zeros_like(col_sum)
    plain[...] = jnp.zeros_like(plain)
    spread[...] = jnp.zeros_like(spread)

    for part, ref in enumerate((own_ref, got_ref)):
        for r in range(half):
            where = part * half + r
            chunk, lanes = where // 2, slice(where % 2 * LANES, (where % 2 + 1) * LANES)
            block = ref[r]
            plain[chunk, 0:terms, lanes] = block
            plain[chunk, LANES : LANES + terms, lanes] = block
            buf = where % 2
            spread[buf, 0:terms, :] = block.astype(F32)
            stage[buf, 0:LANES, :] = spread[buf].T
            pieces = [stage[buf, pl.ds(start, BLK // 2, stride=2), :] for start in (0, 1, BLK, BLK + 1)]
            sorted_rows = jnp.concatenate(pieces, 0)
            turned[2 * where] = sorted_rows[0:BLK].astype(BF)
            turned[2 * where + 1] = sorted_rows[BLK:].astype(BF)
            back = sorted_rows.T.astype(BF)
            mixed[chunk, 0:LANES, lanes] = back
            mixed[chunk, LANES:, lanes] = back

    low_r = low_lanes(tall)
    low_l = low_lanes(2 * rows)

    @pl.loop(0, half)
    def _(chunk):
        weights = plain[chunk]
        for p in range(pairs):
            found = jnp.dot(
                gram_ref[2 * rows * p : 2 * rows * p + 2 * rows + 16, :], weights, preferred_element_type=F32
            )
            for side in range(2):
                first = found[0:tall, side * LANES : (side + 1) * LANES]
                second = found[rows : rows + tall, side * LANES : (side + 1) * LANES]
                lanes = slice(p * LANES, (p + 1) * LANES)
                block = 4 * chunk + 2 * side
                right[block, :, lanes] = jnp.where(low_r, first, pltpu.roll(second, BLK, 1)).astype(BF)
                right[block + 1, :, lanes] = jnp.where(low_r, pltpu.roll(first, BLK, 1), second).astype(BF)
        weights = mixed[chunk]
        for p in range(0, pairs, 2):
            found = jnp.dot(gram_ref[2 * rows * p : 2 * rows * (p + 2), :], weights, preferred_element_type=F32)
            for side in range(2):
                first = found[0 : 2 * rows, side * LANES : (side + 1) * LANES]
                second = found[2 * rows :, side * LANES : (side + 1) * LANES]
                lanes = slice(p * BLK, p * BLK + LANES)
                block = 4 * chunk + 2 * side
                left[block, :, lanes] = jnp.where(low_l, first, pltpu.roll(second, BLK, 1)).astype(BF)
                left[block + 1, :, lanes] = jnp.where(low_l, pltpu.roll(first, BLK, 1), second).astype(BF)

    row_pos = lax.broadcasted_iota(jnp.int32, (BLK, LANES), 0)
    row_dish = row_pos % (BLK // 2) * 2 + row_pos // (BLK // 2)
    ahead = lax.broadcasted_iota(jnp.int32, (BLK, LANES), 1) % BLK - row_dish
    low = low_lanes(BLK // 2)
    here = lax.axis_index("tile") if relative_bits else 0

    def place(block):
        if not relative_bits:
            return block
        return 2 * reverse_bits((block >> 1) ^ here, relative_bits) + (block & 1)

    @pl.loop(0, n_groups)
    def _(group):
        added = []
        for u in range(unroll):
            slot = group * unroll + u
            row, col = rows_ref[slot], cols_ref[slot]
            a, b = place(row), place(col)
            least = jnp.where(slot < count, jnp.where(row == col, 0, -BLK), BLK)
            keep = ahead > least
            fetch(slot).wait()
            for c in range(BLK // 2):
                stage[u, c * channels : (c + 1) * channels, :] = vis[
                    slot, :, c * LANES : (c + 1) * LANES
                ].astype(F32)
            model = jnp.dot(turned[a][:, 0:tall], right[b], preferred_element_type=F32)
            residual = []
            for p in range(pairs):
                first = stage[u, pl.ds(2 * p, BLK // 2, stride=channels), :]
                second = stage[u, pl.ds(2 * p + 1, BLK // 2, stride=channels), :]
                seen = jnp.concatenate(
                    [
                        jnp.where(low, first, pltpu.roll(second, BLK, 1)),
                        jnp.where(low, pltpu.roll(first, BLK, 1), second),
                    ],
                    0,
                )
                difference = model[:, p * LANES : (p + 1) * LANES] - seen
                residual.append(jnp.where(keep, difference, 0.0).astype(BF))
            to_row = lax.dot_general(
                jnp.concatenate(residual, 1), right[b], NT, preferred_element_type=F32
            )
            to_col = jnp.dot(left[a], jnp.concatenate(residual, 0), preferred_element_type=F32)
            added.append((a, b, to_row, to_col))
        for a, b, to_row, to_col in added:
            row_sum[a, :, 0:tall] += to_row
            col_sum[b] += to_col

    low_out = low_lanes(rows)
    for where in range(2 * half):
        buf = where % 2
        for side in range(2):
            total = row_sum[2 * where + side]
            stage[buf, pl.ds(side * BLK, BLK // 2, stride=2), :] = total[0 : BLK // 2]
            stage[buf, pl.ds(side * BLK + 1, BLK // 2, stride=2), :] = total[BLK // 2 :]
        from_rows = stage[buf, 0:LANES, :].T[0:rows]
        cols = []
        for side in range(2):
            total = col_sum[2 * where + side]
            cols.append(total[0:rows] + pltpu.roll(total[rows:], BLK, 1))
        from_cols = jnp.where(low_out, cols[0], pltpu.roll(cols[1], BLK, 1))
        result = ((from_rows + from_cols) * scale)[0:terms]
        if where < half:
            keep_ref[where] = result
        else:
            send_ref[where - half] = result


def tile_terms(relative_bits, scale, tile_count, tile_rows, tile_cols, own, got, gram, observed):
    slots, channels, _ = observed.shape
    half, terms, _ = own.shape
    rows, tall = up(terms, 8), up(terms, 16)
    blocks = 4 * half
    unroll = next(u for u in (2, 3, 1) if slots % u == 0)
    smem = pl.BlockSpec(memory_space=pltpu.SMEM)
    vmem = pl.BlockSpec(memory_space=pltpu.VMEM)
    out = jax.ShapeDtypeStruct((half, terms, LANES), F32)
    return pl.pallas_call(
        functools.partial(tiles_kernel, relative_bits, unroll, scale),
        out_shape=(out, out),
        in_specs=[smem, smem, smem, vmem, vmem, vmem, pl.BlockSpec(memory_space=pl.ANY)],
        out_specs=(vmem, vmem),
        scratch_shapes=[
            pltpu.VMEM((slots, channels, BLK * BLK), BF),
            pltpu.VMEM((max(unroll, 2), channels * BLK // 2, LANES), F32),
            pltpu.VMEM((2, LANES, LANES), F32),
            pltpu.VMEM((half, 2 * LANES, 2 * LANES), BF),
            pltpu.VMEM((half, 2 * LANES, 2 * LANES), BF),
            pltpu.VMEM((blocks, BLK, LANES), BF),
            pltpu.VMEM((blocks, tall, channels * BLK), BF),
            pltpu.VMEM((blocks, 2 * rows, channels // 2 * BLK), BF),
            pltpu.VMEM((blocks, BLK, LANES), F32),
            pltpu.VMEM((blocks, 2 * rows, LANES), F32),
            pltpu.SemaphoreType.DMA((slots,)),
        ],
        compiler_params=pltpu.CompilerParams(vmem_limit_bytes=48 << 20),
        cost_estimate=pl.CostEstimate(
            flops=6 * slots * channels * BLK * BLK * terms, bytes_accessed=observed.size * 2, transcendentals=0
        ),
    )(tile_count, tile_rows, tile_cols, own, got, gram, observed)


def from_partner(array, bit):
    return lax.ppermute(array, "tile", [(i, i ^ 1 << bit) for i in range(lax.axis_size("tile"))])


def on_device(
    coefficients, zernike_table, positions, source_flux, observed, tile_rows, tile_cols, tile_count
):
    members = lax.axis_size("tile")
    terms, shard = coefficients.shape
    dishes = members * shard
    scale = 1.0 / math.sqrt(dishes * positions.shape[0])
    gram = gram_of(zernike_table, positions, source_flux)
    bits = members.bit_length() - 1
    if shard == LANES and members == 1 << bits:
        held = coefficients[None]
        for bit in reversed(range(1, bits)):
            held = jnp.concatenate([held, from_partner(held, bit)], 0)
        got = from_partner(held, 0)
        total, sent = tile_terms(
            bits, scale, tile_count, tile_rows, tile_cols, held, got, gram, observed
        )
        total = total + from_partner(sent, 0)
        for bit in range(1, bits):
            half = total.shape[0] // 2
            total = total[:half] + from_partner(total[half:], bit)
        return total[0]
    everything = lax.all_gather(coefficients, "tile", axis=1, tiled=True)
    everything = everything.reshape(terms, dishes // LANES, LANES).transpose(1, 0, 2)
    half = everything.shape[0] // 2
    parts = tile_terms(
        0, scale, tile_count, tile_rows, tile_cols, everything[:half], everything[half:], gram, observed
    )
    total = jnp.concatenate(parts, 0).transpose(1, 0, 2).reshape(terms, dishes)
    return lax.psum_scatter(total, "tile", scatter_dimension=1, tiled=True)


def solution(mesh):
    return jax.shard_map(
        on_device,
        mesh=mesh,
        in_specs=(
            P(None, "tile"),
            P(),
            P("scan", None),
            P("scan", None),
            P(("scan", "tile"), None, None),
            P(("scan", "tile")),
            P(("scan", "tile")),
            P(("scan", "tile")),
        ),
        out_specs=P("scan", "tile"),
        check_vma=False,
    )
```

```python
import functools
import math

import jax
import jax.numpy as jnp
from jax import lax
from jax.experimental import pallas as pl
from jax.experimental.pallas import tpu as pltpu
from jax.sharding import PartitionSpec as P

BLK = 64
UNROLL = 7
LANES = 128
PIXELS = 256
BF = jnp.bfloat16
F32 = jnp.float32
NT = (((1,), (1,)), ((), ()))


def up(size, unit):
    return -(-size // unit) * unit


def low_lanes(rows):
    return lax.broadcasted_iota(jnp.int32, (rows, LANES), 1) < BLK


def gram_kernel(root, start, count, table_ref, pos_ref, flux_ref, out_ref, groups, gram):
    terms, pixels = table_ref.shape
    sources = pos_ref.shape[1]
    n_groups = pixels // PIXELS
    tall = groups.shape[0] // n_groups
    rows = up(terms, 8)
    groups[...] = jnp.zeros_like(groups)
    gram[...] = jnp.zeros_like(gram)
    for h in range(n_groups):
        groups[h * tall : h * tall + terms, :] = table_ref[:, h * PIXELS : (h + 1) * PIXELS]
    pixel = lax.broadcasted_iota(jnp.int32, (PIXELS, sources), 0)
    for f in range(count):
        pos = pos_ref[start + f : start + f + 1, :]
        hot = jnp.where(pixel == pos % PIXELS, 1.0, 0.0).astype(BF)
        found = jnp.dot(groups[...], hot, preferred_element_type=F32)
        group = pos // PIXELS
        chosen = jnp.zeros((tall, sources), F32)
        for h in range(n_groups):
            chosen = jnp.where(group == h, found[h * tall : (h + 1) * tall], chosen)
        scaled = chosen * (flux_ref[start + f : start + f + 1, :] / root)
        high = scaled.astype(BF)
        low = (scaled - high.astype(F32)).astype(BF)
        chosen = chosen.astype(BF)
        product = lax.dot_general(high, chosen, NT, preferred_element_type=F32)
        product = product + lax.dot_general(low, chosen, NT, preferred_element_type=F32)
        gram[f * rows : f * rows + tall, 0:tall] = product
    value = gram[...]
    high = value.astype(BF)
    out_ref[:, 0:LANES] = high
    out_ref[:, LANES : 2 * LANES] = (value - high.astype(F32)).astype(BF)


def gram_of(zernike_table, positions, source_flux, start, count):
    terms, pixels = zernike_table.shape
    sources = positions.shape[1]
    rows, tall = up(terms, 8), up(terms, 16)
    height = up(count * rows + 8, 16)
    return pl.pallas_call(
        functools.partial(gram_kernel, math.sqrt(sources), start, count),
        out_shape=jax.ShapeDtypeStruct((height, 2 * LANES), BF),
        in_specs=[pl.BlockSpec(memory_space=pltpu.VMEM)] * 3,
        out_specs=pl.BlockSpec(memory_space=pltpu.VMEM),
        scratch_shapes=[
            pltpu.VMEM((pixels // PIXELS * tall, PIXELS), BF),
            pltpu.VMEM((height, LANES), F32),
        ],
        compiler_params=pltpu.CompilerParams(vmem_limit_bytes=32 << 20),
        cost_estimate=pl.CostEstimate(
            flops=2 * count * sources * pixels * terms, bytes_accessed=1 << 20, transcendentals=0
        ),
    )(zernike_table, positions, source_flux)


def reverse_bits(value, bits):
    result = value & 0
    for bit in range(bits):
        result = result | ((value >> bit) & 1) << (bits - 1 - bit)
    return result


def tiles_kernel(
    relative_bits, unroll, scale,
    mine_ref, other_ref, own_ref, got_ref, first_gram_ref, second_gram_ref, vis_hbm, more_hbm,
    keep_ref, send_ref,
    vis, stage, spread, both, turned, right, left, row_sum, col_sum, sems,
):
    slots, channels = vis.shape[0], vis.shape[1]
    kept = slots - more_hbm.shape[0]
    half, terms = own_ref.shape[0], own_ref.shape[1]
    pairs = channels // 2
    rows, tall = up(terms, 8), up(terms, 16)
    n_mine = jnp.minimum(mine_ref[2 * slots], kept)
    n_live = n_mine + jnp.maximum(other_ref[2 * slots] - kept, 0)
    copies = (
        pltpu.make_async_copy(vis_hbm.at[pl.ds(0, kept)], vis.at[pl.ds(0, kept)], sems.at[0]),
        pltpu.make_async_copy(more_hbm, vis.at[pl.ds(kept, slots - kept)], sems.at[1]),
    )
    for copy in copies:
        copy.start()

    row_sum[...] = jnp.zeros_like(row_sum)
    col_sum[...] = jnp.zeros_like(col_sum)
    both[...] = jnp.zeros_like(both)
    spread[...] = jnp.zeros_like(spread)

    for part, ref in enumerate((own_ref, got_ref)):
        for r in range(half):
            where = part * half + r
            chunk, lanes = where // 2, slice(where % 2 * LANES, (where % 2 + 1) * LANES)
            block = ref[r]
            both[chunk, 0:terms, lanes] = block
            both[chunk, LANES : LANES + terms, lanes] = block
            buf = where % 2
            spread[buf, 0:terms, :] = block.astype(F32)
            stage[buf, 0:LANES, :] = spread[buf].T
            pieces = [stage[buf, pl.ds(start, BLK // 2, stride=2), :] for start in (0, 1, BLK, BLK + 1)]
            sorted_rows = jnp.concatenate(pieces, 0)
            turned[2 * where] = sorted_rows[0:BLK].astype(BF)
            turned[2 * where + 1] = sorted_rows[BLK:].astype(BF)
            back = sorted_rows.T.astype(BF)
            lanes = slice((where % 2 + 2) * LANES, (where % 2 + 3) * LANES)
            both[chunk, 0:LANES, lanes] = back
            both[chunk, LANES:, lanes] = back

    low_r = low_lanes(tall)
    low_l = low_lanes(2 * rows)

    @pl.loop(0, half)
    def _(chunk):
        weights = both[chunk]
        for p in range(0, pairs, 2):
            gram_ref = first_gram_ref if p < pairs // 2 else second_gram_ref
            start = p % (pairs // 2) * 2 * rows
            found = jnp.dot(
                gram_ref[start : start + 4 * rows + 16, :], weights, preferred_element_type=F32
            )
            for side in range(2):
                block = 4 * chunk + 2 * side
                part = found[:, side * LANES : (side + 1) * LANES]
                for e in range(2):
                    first = part[2 * e * rows : 2 * e * rows + tall]
                    second = part[(2 * e + 1) * rows : (2 * e + 1) * rows + tall]
                    lanes = slice((p + e) * LANES, (p + e + 1) * LANES)
                    right[block, :, lanes] = jnp.where(low_r, first, pltpu.roll(second, BLK, 1)).astype(BF)
                    right[block + 1, :, lanes] = jnp.where(low_r, pltpu.roll(first, BLK, 1), second).astype(BF)
                part = found[:, (side + 2) * LANES : (side + 3) * LANES]
                first, second = part[0 : 2 * rows], part[2 * rows : 4 * rows]
                lanes = slice(p * BLK, p * BLK + LANES)
                left[block, :, lanes] = jnp.where(low_l, first, pltpu.roll(second, BLK, 1)).astype(BF)
                left[block + 1, :, lanes] = jnp.where(low_l, pltpu.roll(first, BLK, 1), second).astype(BF)

    row_pos = lax.broadcasted_iota(jnp.int32, (BLK, LANES), 0)
    row_dish = row_pos % (BLK // 2) * 2 + row_pos // (BLK // 2)
    ahead = lax.broadcasted_iota(jnp.int32, (BLK, LANES), 1) % BLK - row_dish
    low = low_lanes(BLK // 2)
    here = lax.axis_index("tile") if relative_bits else 0

    def place(block):
        if not relative_bits:
            return block
        return 2 * reverse_bits((block >> 1) ^ here, relative_bits) + (block & 1)

    for copy in copies:
        copy.wait()

    @pl.loop(0, (n_live + unroll - 1) // unroll)
    def _(group):
        slot_ids, pairs_of, leasts = [], [], []
        for u in range(unroll):
            turn = group * unroll + u
            is_mine = turn < n_mine
            slot = jnp.minimum(jnp.where(is_mine, turn, kept + turn - n_mine), slots - 1)
            row = jnp.where(is_mine, mine_ref[slot], other_ref[slot])
            col = jnp.where(is_mine, mine_ref[slots + slot], other_ref[slots + slot])
            slot_ids.append(slot)
            pairs_of.append((place(row), place(col)))
            leasts.append(jnp.where(turn < n_live, jnp.where(row == col, 0, -BLK), BLK))
        for u, slot in enumerate(slot_ids):
            for c in range(BLK // 2):
                stage[u, c * channels : (c + 1) * channels, :] = vis[
                    slot, :, c * LANES : (c + 1) * LANES
                ].astype(F32)
        models = [
            jnp.dot(turned[a][:, 0:tall], right[b], preferred_element_type=F32) for a, b in pairs_of
        ]
        residuals = []
        for u, slot in enumerate(slot_ids):
            keep = ahead > leasts[u]
            residual = []
            for p in range(pairs):
                first = stage[u, pl.ds(2 * p, BLK // 2, stride=channels), :]
                second = stage[u, pl.ds(2 * p + 1, BLK // 2, stride=channels), :]
                seen = jnp.concatenate(
                    [
                        jnp.where(low, first, pltpu.roll(second, BLK, 1)),
                        jnp.where(low, pltpu.roll(first, BLK, 1), second),
                    ],
                    0,
                )
                difference = models[u][:, p * LANES : (p + 1) * LANES] - seen
                residual.append(jnp.where(keep, difference, 0.0).astype(BF))
            residuals.append(residual)
        to_rows = [
            lax.dot_general(jnp.concatenate(residual, 1), right[b], NT, preferred_element_type=F32)
            for (a, b), residual in zip(pairs_of, residuals)
        ]
        to_cols = [
            jnp.dot(left[a], jnp.concatenate(residual, 0), preferred_element_type=F32)
            for (a, b), residual in zip(pairs_of, residuals)
        ]
        for (a, b), to_row, to_col in zip(pairs_of, to_rows, to_cols):
            row_sum[a, :, 0:tall] += to_row
            col_sum[b] += to_col

    low_out = low_lanes(rows)
    for where in range(2 * half):
        buf = where % 2
        for side in range(2):
            total = row_sum[2 * where + side]
            stage[buf, pl.ds(side * BLK, BLK // 2, stride=2), :] = total[0 : BLK // 2]
            stage[buf, pl.ds(side * BLK + 1, BLK // 2, stride=2), :] = total[BLK // 2 :]
        from_rows = stage[buf, 0:LANES, :].T[0:rows]
        cols = []
        for side in range(2):
            total = col_sum[2 * where + side]
            cols.append(total[0:rows] + pltpu.roll(total[rows:], BLK, 1))
        from_cols = jnp.where(low_out, cols[0], pltpu.roll(cols[1], BLK, 1))
        result = ((from_rows + from_cols) * scale)[0:terms]
        if where < half:
            keep_ref[where] = result
        else:
            send_ref[where - half] = result


def tile_terms(relative_bits, scale, mine, other, own, got, grams, observed, more):
    slots, channels, _ = observed.shape
    half, terms, _ = own.shape
    rows, tall = up(terms, 8), up(terms, 16)
    blocks = 4 * half
    unroll = UNROLL
    smem = pl.BlockSpec(memory_space=pltpu.SMEM)
    vmem = pl.BlockSpec(memory_space=pltpu.VMEM)
    out = jax.ShapeDtypeStruct((half, terms, LANES), F32)
    return pl.pallas_call(
        functools.partial(tiles_kernel, relative_bits, unroll, scale),
        out_shape=(out, out),
        in_specs=[smem, smem, vmem, vmem, vmem, vmem] + [pl.BlockSpec(memory_space=pl.ANY)] * 2,
        out_specs=(vmem, vmem),
        scratch_shapes=[
            pltpu.VMEM((slots, channels, BLK * BLK), BF),
            pltpu.VMEM((max(unroll, 2), channels * BLK // 2, LANES), F32),
            pltpu.VMEM((2, LANES, LANES), F32),
            pltpu.VMEM((half, 2 * LANES, 4 * LANES), BF),
            pltpu.VMEM((blocks, BLK, LANES), BF),
            pltpu.VMEM((blocks, tall, channels * BLK), BF),
            pltpu.VMEM((blocks, 2 * rows, channels // 2 * BLK), BF),
            pltpu.VMEM((blocks, BLK, LANES), F32),
            pltpu.VMEM((blocks, 2 * rows, LANES), F32),
            pltpu.SemaphoreType.DMA((2,)),
        ],
        compiler_params=pltpu.CompilerParams(vmem_limit_bytes=48 << 20),
        cost_estimate=pl.CostEstimate(
            flops=6 * slots * channels * BLK * BLK * terms, bytes_accessed=observed.size * 2, transcendentals=0
        ),
    )(mine, other, own, got, *grams, observed, more)


def from_partner(array, bit):
    return lax.ppermute(array, "tile", [(i, i ^ 1 << bit) for i in range(lax.axis_size("tile"))])


def on_device(
    coefficients, zernike_table, positions, source_flux, observed, tile_rows, tile_cols, tile_count
):
    members = lax.axis_size("tile")
    terms, shard = coefficients.shape
    dishes = members * shard
    scale = 1.0 / math.sqrt(dishes * positions.shape[0])
    channels, slots = positions.shape[0], tile_rows.shape[0]
    bits = members.bit_length() - 1
    moved = slots // 4 + 1
    mine = jnp.concatenate([tile_rows, tile_cols, tile_count])
    other = from_partner(mine, 0)
    more = from_partner(observed[slots - moved :], 0)
    grams = [
        gram_of(zernike_table, positions, source_flux, start, channels // 2)
        for start in (0, channels // 2)
    ]
    if shard == LANES and members == 1 << bits:
        held = coefficients[None]
        for step, bit in enumerate(reversed(range(1, bits))):
            held = jnp.concatenate([held, from_partner(held, bit)], 0)
            if step < 2:
                held, grams[step] = lax.optimization_barrier((held, grams[step]))
        got = from_partner(held, 0)
        total, sent = tile_terms(bits, scale, mine, other, held, got, grams, observed, more)
        total = total + from_partner(sent, 0)
        for bit in range(1, bits):
            half = total.shape[0] // 2
            total = total[:half] + from_partner(total[half:], bit)
        return total[0]
    everything = lax.all_gather(coefficients, "tile", axis=1, tiled=True)
    everything = everything.reshape(terms, dishes // LANES, LANES).transpose(1, 0, 2)
    half = everything.shape[0] // 2
    parts = tile_terms(
        0, scale, mine, other, everything[:half], everything[half:], grams, observed, more
    )
    total = jnp.concatenate(parts, 0).transpose(1, 0, 2).reshape(terms, dishes)
    return lax.psum_scatter(total, "tile", scatter_dimension=1, tiled=True)


def solution(mesh):
    return jax.shard_map(
        on_device,
        mesh=mesh,
        in_specs=(
            P(None, "tile"),
            P(),
            P("scan", None),
            P("scan", None),
            P(("scan", "tile"), None, None),
            P(("scan", "tile")),
            P(("scan", "tile")),
            P(("scan", "tile")),
        ),
        out_specs=P("scan", "tile"),
        check_vma=False,
    )
```

```python
import functools
import math

import jax
import jax.numpy as jnp
from jax import lax
from jax.experimental import pallas as pl
from jax.experimental.pallas import tpu as pltpu
from jax.sharding import PartitionSpec as P

BLK = 64
UNROLL = 7
LANES = 128
PIXELS = 256
BF = jnp.bfloat16
F32 = jnp.float32
NT = (((1,), (1,)), ((), ()))


def up(size, unit):
    return -(-size // unit) * unit


def low_lanes(rows):
    return lax.broadcasted_iota(jnp.int32, (rows, LANES), 1) < BLK


def gram_kernel(root, start, count, table_ref, pos_ref, flux_ref, *rest):
    if len(rest) > 3:
        vis_hbm, out_ref, moved_hbm, groups, gram, sem = rest
        moved = moved_hbm.shape[0]
        copy = pltpu.make_async_copy(vis_hbm.at[pl.ds(vis_hbm.shape[0] - moved, moved)], moved_hbm, sem)
        copy.start()
    else:
        out_ref, groups, gram = rest
        copy = None
    terms, pixels = table_ref.shape
    sources = pos_ref.shape[1]
    n_groups = pixels // PIXELS
    tall = groups.shape[0] // n_groups
    rows = up(terms, 8)
    groups[...] = jnp.zeros_like(groups)
    gram[...] = jnp.zeros_like(gram)
    for h in range(n_groups):
        groups[h * tall : h * tall + terms, :] = table_ref[:, h * PIXELS : (h + 1) * PIXELS]
    pixel = lax.broadcasted_iota(jnp.int32, (PIXELS, sources), 0)
    for f in range(count):
        pos = pos_ref[start + f : start + f + 1, :]
        hot = jnp.where(pixel == pos % PIXELS, 1.0, 0.0).astype(BF)
        found = jnp.dot(groups[...], hot, preferred_element_type=F32)
        group = pos // PIXELS
        chosen = jnp.zeros((tall, sources), F32)
        for h in range(n_groups):
            chosen = jnp.where(group == h, found[h * tall : (h + 1) * tall], chosen)
        scaled = chosen * (flux_ref[start + f : start + f + 1, :] / root)
        high = scaled.astype(BF)
        low = (scaled - high.astype(F32)).astype(BF)
        chosen = chosen.astype(BF)
        product = lax.dot_general(high, chosen, NT, preferred_element_type=F32)
        product = product + lax.dot_general(low, chosen, NT, preferred_element_type=F32)
        gram[f * rows : f * rows + tall, 0:tall] = product
    value = gram[...]
    high = value.astype(BF)
    out_ref[:, 0:LANES] = high
    out_ref[:, LANES : 2 * LANES] = (value - high.astype(F32)).astype(BF)
    if copy is not None:
        copy.wait()


def gram_of(zernike_table, positions, source_flux, start, count, observed=None, moved=0):
    terms, pixels = zernike_table.shape
    sources = positions.shape[1]
    rows, tall = up(terms, 8), up(terms, 16)
    height = up(count * rows + 8, 16)
    vmem = pl.BlockSpec(memory_space=pltpu.VMEM)
    anywhere = pl.BlockSpec(memory_space=pl.ANY)
    out_shape = [jax.ShapeDtypeStruct((height, 2 * LANES), BF)]
    scratch = [pltpu.VMEM((pixels // PIXELS * tall, PIXELS), BF), pltpu.VMEM((height, LANES), F32)]
    operands, in_specs, out_specs = [zernike_table, positions, source_flux], [vmem] * 3, [vmem]
    if moved:
        operands.append(observed)
        in_specs.append(anywhere)
        out_shape.append(jax.ShapeDtypeStruct((moved,) + observed.shape[1:], BF))
        out_specs.append(anywhere)
        scratch.append(pltpu.SemaphoreType.DMA)
    return pl.pallas_call(
        functools.partial(gram_kernel, math.sqrt(sources), start, count),
        out_shape=out_shape,
        in_specs=in_specs,
        out_specs=out_specs,
        scratch_shapes=scratch,
        compiler_params=pltpu.CompilerParams(vmem_limit_bytes=56 << 20),
        cost_estimate=pl.CostEstimate(
            flops=2 * count * sources * pixels * terms, bytes_accessed=1 << 20, transcendentals=0
        ),
    )(*operands)


def relative_place(device, here):
    apart = device ^ here
    near, far = (apart >> 1) & 1, (apart >> 2) & 1
    odd = (device & 1) == 1
    return (
        8 * (apart & 1)
        + 4 * jnp.where(odd, far, near)
        + 2 * jnp.where(odd, near, far)
        + ((apart >> 3) & 1)
    )


def tiles_kernel(
    relative, unroll, scale, pieces,
    mine_ref, other_ref, own_ref, got_ref, vis_hbm, more_hbm, *rest,
):
    gram_refs, rest = rest[: len(pieces)], rest[len(pieces) :]
    keep_ref, send_ref, vis, stage, spread, both, turned, right, left, row_sum, col_sum, sems = rest
    slots, channels = vis.shape[0], vis.shape[1]
    kept = slots - more_hbm.shape[0]
    half, terms = own_ref.shape[0], own_ref.shape[1]
    pairs = channels // 2
    rows, tall = up(terms, 8), up(terms, 16)
    n_mine = jnp.minimum(mine_ref[2 * slots], kept)
    n_live = n_mine + jnp.maximum(other_ref[2 * slots] - kept, 0)
    copies = (
        pltpu.make_async_copy(vis_hbm.at[pl.ds(0, kept)], vis.at[pl.ds(0, kept)], sems.at[0]),
        pltpu.make_async_copy(more_hbm, vis.at[pl.ds(kept, slots - kept)], sems.at[1]),
    )
    for copy in copies:
        copy.start()

    row_sum[...] = jnp.zeros_like(row_sum)
    col_sum[...] = jnp.zeros_like(col_sum)
    both[...] = jnp.zeros_like(both)
    per_tile = stage.shape[1] // LANES
    spread[...] = jnp.zeros_like(spread)

    for part, ref in enumerate((own_ref, got_ref)):
        for r in range(half):
            where = part * half + r
            chunk, lanes = where // 2, slice(where % 2 * LANES, (where % 2 + 1) * LANES)
            block = ref[r]
            both[chunk, 0:terms, lanes] = block
            both[chunk, LANES : LANES + terms, lanes] = block
            spread[where, 0:terms, :] = block.astype(F32)
            buf, base = where // per_tile, where % per_tile * LANES
            stage[buf, base : base + LANES, :] = spread[where].T
            sorted_rows = jnp.concatenate(
                [
                    stage[buf, pl.ds(base + start, BLK // 2, stride=2), :]
                    for start in (0, 1, BLK, BLK + 1)
                ],
                0,
            )
            turned[2 * where] = sorted_rows[0:BLK].astype(BF)
            turned[2 * where + 1] = sorted_rows[BLK:].astype(BF)
            back = sorted_rows.T.astype(BF)
            lanes = slice((where % 2 + 2) * LANES, (where % 2 + 3) * LANES)
            both[chunk, 0:LANES, lanes] = back
            both[chunk, LANES:, lanes] = back

    low_r = low_lanes(tall)
    low_l = low_lanes(2 * rows)

    @pl.loop(0, half)
    def _(chunk):
        weights = both[chunk]
        for p in range(0, pairs, 2):
            piece = max(n for n, (first, _) in enumerate(pieces) if first <= 2 * p)
            gram_ref, start = gram_refs[piece], (2 * p - pieces[piece][0]) * rows
            found = jnp.dot(
                gram_ref[start : start + 4 * rows + 16, :], weights, preferred_element_type=F32
            )
            for side in range(2):
                block = 4 * chunk + 2 * side
                part = found[:, side * LANES : (side + 1) * LANES]
                for e in range(2):
                    first = part[2 * e * rows : 2 * e * rows + tall]
                    second = part[(2 * e + 1) * rows : (2 * e + 1) * rows + tall]
                    lanes = slice((p + e) * LANES, (p + e + 1) * LANES)
                    right[block, :, lanes] = jnp.where(low_r, first, pltpu.roll(second, BLK, 1)).astype(BF)
                    right[block + 1, :, lanes] = jnp.where(low_r, pltpu.roll(first, BLK, 1), second).astype(BF)
                part = found[:, (side + 2) * LANES : (side + 3) * LANES]
                first, second = part[0 : 2 * rows], part[2 * rows : 4 * rows]
                lanes = slice(p * BLK, p * BLK + LANES)
                left[block, :, lanes] = jnp.where(low_l, first, pltpu.roll(second, BLK, 1)).astype(BF)
                left[block + 1, :, lanes] = jnp.where(low_l, pltpu.roll(first, BLK, 1), second).astype(BF)

    row_pos = lax.broadcasted_iota(jnp.int32, (BLK, LANES), 0)
    row_dish = row_pos % (BLK // 2) * 2 + row_pos // (BLK // 2)
    ahead = lax.broadcasted_iota(jnp.int32, (BLK, LANES), 1) % BLK - row_dish
    low = low_lanes(BLK // 2)
    here = lax.axis_index("tile") if relative else 0

    def place(block):
        return 2 * relative_place(block >> 1, here) + (block & 1) if relative else block

    for copy in copies:
        copy.wait()

    @pl.loop(0, (n_live + unroll - 1) // unroll)
    def _(group):
        slot_ids, pairs_of, leasts = [], [], []
        for u in range(unroll):
            turn = group * unroll + u
            is_mine = turn < n_mine
            slot = jnp.minimum(jnp.where(is_mine, turn, kept + turn - n_mine), slots - 1)
            row = jnp.where(is_mine, mine_ref[slot], other_ref[slot])
            col = jnp.where(is_mine, mine_ref[slots + slot], other_ref[slots + slot])
            slot_ids.append(slot)
            pairs_of.append((place(row), place(col)))
            leasts.append(jnp.where(turn < n_live, jnp.where(row == col, 0, -BLK), BLK))
        for u, slot in enumerate(slot_ids):
            for c in range(BLK // 2):
                stage[u, c * channels : (c + 1) * channels, :] = vis[
                    slot, :, c * LANES : (c + 1) * LANES
                ].astype(F32)
        models = [
            jnp.dot(turned[a][:, 0:tall], right[b], preferred_element_type=F32) for a, b in pairs_of
        ]
        residuals = []
        for u, slot in enumerate(slot_ids):
            keep = ahead > leasts[u]
            residual = []
            for p in range(pairs):
                first = stage[u, pl.ds(2 * p, BLK // 2, stride=channels), :]
                second = stage[u, pl.ds(2 * p + 1, BLK // 2, stride=channels), :]
                seen = jnp.concatenate(
                    [
                        jnp.where(low, first, pltpu.roll(second, BLK, 1)),
                        jnp.where(low, pltpu.roll(first, BLK, 1), second),
                    ],
                    0,
                )
                difference = models[u][:, p * LANES : (p + 1) * LANES] - seen
                residual.append(jnp.where(keep, difference, 0.0).astype(BF))
            residuals.append(residual)
        to_rows = [
            lax.dot_general(jnp.concatenate(residual, 1), right[b], NT, preferred_element_type=F32)
            for (a, b), residual in zip(pairs_of, residuals)
        ]
        to_cols = [
            jnp.dot(left[a], jnp.concatenate(residual, 0), preferred_element_type=F32)
            for (a, b), residual in zip(pairs_of, residuals)
        ]
        for (a, b), to_row, to_col in zip(pairs_of, to_rows, to_cols):
            row_sum[a, :, 0:tall] += to_row
            col_sum[b] += to_col

    low_out = low_lanes(rows)
    for where in range(2 * half):
        buf, base = where // per_tile, where % per_tile * LANES
        for side in range(2):
            total = row_sum[2 * where + side]
            start = base + side * BLK
            stage[buf, pl.ds(start, BLK // 2, stride=2), :] = total[0 : BLK // 2]
            stage[buf, pl.ds(start + 1, BLK // 2, stride=2), :] = total[BLK // 2 :]
    for where in range(2 * half):
        buf, base = where // per_tile, where % per_tile * LANES
        from_rows = stage[buf, base : base + LANES, :].T[0:rows]
        cols = []
        for side in range(2):
            total = col_sum[2 * where + side]
            cols.append(total[0:rows] + pltpu.roll(total[rows:], BLK, 1))
        from_cols = jnp.where(low_out, cols[0], pltpu.roll(cols[1], BLK, 1))
        result = ((from_rows + from_cols) * scale)[0:terms]
        if where < half:
            keep_ref[where] = result
        else:
            send_ref[where - half] = result


def tile_terms(relative, scale, pieces, mine, other, own, got, grams, observed, more):
    slots, channels, _ = observed.shape
    half, terms, _ = own.shape
    rows, tall = up(terms, 8), up(terms, 16)
    blocks = 4 * half
    unroll = UNROLL
    smem = pl.BlockSpec(memory_space=pltpu.SMEM)
    vmem = pl.BlockSpec(memory_space=pltpu.VMEM)
    out = jax.ShapeDtypeStruct((half, terms, LANES), F32)
    return pl.pallas_call(
        functools.partial(tiles_kernel, relative, unroll, scale, pieces),
        out_shape=(out, out),
        in_specs=[smem, smem, vmem, vmem] + [pl.BlockSpec(memory_space=pl.ANY)] * 2 + [vmem] * len(grams),
        out_specs=(vmem, vmem),
        scratch_shapes=[
            pltpu.VMEM((slots, channels, BLK * BLK), BF),
            pltpu.VMEM((up(max(unroll, 2 * half * LANES // (channels * BLK // 2)), 1), channels * BLK // 2, LANES), F32),
            pltpu.VMEM((2 * half, LANES, LANES), F32),
            pltpu.VMEM((half, 2 * LANES, 4 * LANES), BF),
            pltpu.VMEM((blocks, BLK, LANES), BF),
            pltpu.VMEM((blocks, tall, channels * BLK), BF),
            pltpu.VMEM((blocks, 2 * rows, channels // 2 * BLK), BF),
            pltpu.VMEM((blocks, BLK, LANES), F32),
            pltpu.VMEM((blocks, 2 * rows, LANES), F32),
            pltpu.SemaphoreType.DMA((2,)),
        ],
        compiler_params=pltpu.CompilerParams(vmem_limit_bytes=48 << 20),
        cost_estimate=pl.CostEstimate(
            flops=6 * slots * channels * BLK * BLK * terms, bytes_accessed=observed.size * 2, transcendentals=0
        ),
    )(mine, other, own, got, observed, more, *grams)


def from_partner(array, even, odd=None):
    odd = even if odd is None else odd
    return lax.ppermute(
        array, "tile", [(i, i ^ (odd if i % 2 else even)) for i in range(lax.axis_size("tile"))]
    )


def on_device(
    coefficients, zernike_table, positions, source_flux, observed, tile_rows, tile_cols, tile_count
):
    members = lax.axis_size("tile")
    terms, shard = coefficients.shape
    dishes = members * shard
    scale = 1.0 / math.sqrt(dishes * positions.shape[0])
    channels, slots = positions.shape[0], tile_rows.shape[0]
    moved = slots // 4 + 1
    mine = jnp.concatenate([tile_rows, tile_cols, tile_count])
    other = from_partner(mine, 1)
    quarter = channels // 4
    pieces = ((0, 2 * quarter), (2 * quarter, quarter), (3 * quarter, quarter))
    first, to_move = gram_of(zernike_table, positions, source_flux, *pieces[0], observed, moved)
    grams = [first] + [
        gram_of(zernike_table, positions, source_flux, *piece)[0] for piece in pieces[1:]
    ]
    if shard == LANES and members == 16:
        held = coefficients[None]
        held = jnp.concatenate([held, from_partner(held, 8)], 0)
        held, grams[0], to_move, other = lax.optimization_barrier((held, grams[0], to_move, other))
        more = from_partner(to_move, 1)
        held = jnp.concatenate([held, from_partner(held, 4, 2)], 0)
        held, grams[1] = lax.optimization_barrier((held, grams[1]))
        held = jnp.concatenate([held, from_partner(held, 2, 4)], 0)
        held, grams[2] = lax.optimization_barrier((held, grams[2]))
        got = from_partner(held, 1)
        total, sent = tile_terms(
            True, scale, pieces, mine, other, held, got, grams, observed, more
        )
        total = total + from_partner(sent, 1)
        total = total[:4] + from_partner(total[4:], 2, 4)
        total = total[:2] + from_partner(total[2:], 4, 2)
        total = total[:1] + from_partner(total[1:], 8)
        return total[0]
    more = from_partner(to_move, 1)
    everything = lax.all_gather(coefficients, "tile", axis=1, tiled=True)
    everything = everything.reshape(terms, dishes // LANES, LANES).transpose(1, 0, 2)
    half = everything.shape[0] // 2
    parts = tile_terms(
        False, scale, pieces, mine, other, everything[:half], everything[half:], grams, observed, more
    )
    total = jnp.concatenate(parts, 0).transpose(1, 0, 2).reshape(terms, dishes)
    return lax.psum_scatter(total, "tile", scatter_dimension=1, tiled=True)


def solution(mesh):
    return jax.shard_map(
        on_device,
        mesh=mesh,
        in_specs=(
            P(None, "tile"),
            P(),
            P("scan", None),
            P("scan", None),
            P(("scan", "tile"), None, None),
            P(("scan", "tile")),
            P(("scan", "tile")),
            P(("scan", "tile")),
        ),
        out_specs=P("scan", "tile"),
        check_vma=False,
    )
```

```python
import functools
import math

import jax
import jax.numpy as jnp
from jax import lax
from jax.experimental import pallas as pl
from jax.experimental.pallas import tpu as pltpu
from jax.sharding import PartitionSpec as P

BLK = 64
UNROLL = 7
LANES = 128
PIXELS = 256
BF = jnp.bfloat16
F32 = jnp.float32
NT = (((1,), (1,)), ((), ()))


def up(size, unit):
    return -(-size // unit) * unit


def low_lanes(rows):
    return lax.broadcasted_iota(jnp.int32, (rows, LANES), 1) < BLK


def gram_kernel(root, table_ref, pos_ref, flux_ref, out_ref, groups, gram):
    terms, pixels = table_ref.shape
    channels, sources = pos_ref.shape
    count = channels // 2
    start = lax.axis_index("tile") % 2 * count
    n_groups = pixels // PIXELS
    tall = groups.shape[0] // n_groups
    rows = up(terms, 8)
    groups[...] = jnp.zeros_like(groups)
    gram[...] = jnp.zeros_like(gram)
    for h in range(n_groups):
        groups[h * tall : h * tall + terms, :] = table_ref[:, h * PIXELS : (h + 1) * PIXELS]
    pixel = lax.broadcasted_iota(jnp.int32, (PIXELS, sources), 0)
    for f in range(count):
        pos = pos_ref[pl.ds(start + f, 1), :]
        hot = jnp.where(pixel == pos % PIXELS, 1.0, 0.0).astype(BF)
        found = jnp.dot(groups[...], hot, preferred_element_type=F32)
        group = pos // PIXELS
        chosen = jnp.zeros((tall, sources), F32)
        for h in range(n_groups):
            chosen = jnp.where(group == h, found[h * tall : (h + 1) * tall], chosen)
        scaled = chosen * (flux_ref[pl.ds(start + f, 1), :] / root)
        high = scaled.astype(BF)
        low = (scaled - high.astype(F32)).astype(BF)
        chosen = chosen.astype(BF)
        product = lax.dot_general(high, chosen, NT, preferred_element_type=F32)
        product = product + lax.dot_general(low, chosen, NT, preferred_element_type=F32)
        gram[f * rows : f * rows + tall, 0:tall] = product
    value = gram[...]
    high = value.astype(BF)
    out_ref[:, 0:LANES] = high
    out_ref[:, LANES : 2 * LANES] = (value - high.astype(F32)).astype(BF)


def gram_of(zernike_table, positions, source_flux):
    terms, pixels = zernike_table.shape
    channels, sources = positions.shape
    count = channels // 2
    rows, tall = up(terms, 8), up(terms, 16)
    height = up(count * rows + 8, 16)
    return pl.pallas_call(
        functools.partial(gram_kernel, math.sqrt(sources)),
        out_shape=jax.ShapeDtypeStruct((height, 2 * LANES), BF),
        in_specs=[pl.BlockSpec(memory_space=pltpu.VMEM)] * 3,
        out_specs=pl.BlockSpec(memory_space=pltpu.VMEM),
        scratch_shapes=[
            pltpu.VMEM((pixels // PIXELS * tall, PIXELS), BF),
            pltpu.VMEM((height, LANES), F32),
        ],
        compiler_params=pltpu.CompilerParams(vmem_limit_bytes=32 << 20),
        cost_estimate=pl.CostEstimate(
            flops=2 * count * sources * pixels * terms, bytes_accessed=1 << 20, transcendentals=0
        ),
    )(zernike_table, positions, source_flux)


def relative_place(device, here):
    apart = device ^ here
    return 8 * (apart & 1) + (apart & 6) + (apart >> 3)


def tiles_kernel(
    relative, unroll, scale,
    mine_ref, other_ref, own_ref, got_ref, vis_hbm, more_hbm, own_gram_ref, got_gram_ref,
    keep_ref, send_ref,
    vis, stage, spread, both, gram, turned, right, left, row_sum, col_sum, sems,
):
    slots, channels = vis.shape[0], vis.shape[1]
    kept = slots - more_hbm.shape[0]
    half, terms = own_ref.shape[0], own_ref.shape[1]
    pairs = channels // 2
    rows, tall = up(terms, 8), up(terms, 16)
    n_mine = jnp.minimum(mine_ref[2 * slots], kept)
    n_live = n_mine + jnp.maximum(other_ref[2 * slots] - kept, 0)
    copies = (
        pltpu.make_async_copy(vis_hbm.at[pl.ds(0, kept)], vis.at[pl.ds(0, kept)], sems.at[0]),
        pltpu.make_async_copy(more_hbm, vis.at[pl.ds(kept, slots - kept)], sems.at[1]),
    )
    for copy in copies:
        copy.start()

    row_sum[...] = jnp.zeros_like(row_sum)
    col_sum[...] = jnp.zeros_like(col_sum)
    both[...] = jnp.zeros_like(both)
    per_tile = stage.shape[1] // LANES
    spread[...] = jnp.zeros_like(spread)

    for part, ref in enumerate((own_ref, got_ref)):
        for r in range(half):
            where = part * half + r
            chunk, lanes = where // 2, slice(where % 2 * LANES, (where % 2 + 1) * LANES)
            block = ref[r]
            both[chunk, 0:terms, lanes] = block
            both[chunk, LANES : LANES + terms, lanes] = block
            spread[where, 0:terms, :] = block.astype(F32)
            buf, base = where // per_tile, where % per_tile * LANES
            stage[buf, base : base + LANES, :] = spread[where].T
            sorted_rows = jnp.concatenate(
                [
                    stage[buf, pl.ds(base + start, BLK // 2, stride=2), :]
                    for start in (0, 1, BLK, BLK + 1)
                ],
                0,
            )
            turned[2 * where] = sorted_rows[0:BLK].astype(BF)
            turned[2 * where + 1] = sorted_rows[BLK:].astype(BF)
            back = sorted_rows.T.astype(BF)
            lanes = slice((where % 2 + 2) * LANES, (where % 2 + 3) * LANES)
            both[chunk, 0:LANES, lanes] = back
            both[chunk, LANES:, lanes] = back

    here = lax.axis_index("tile")
    gram[here % 2] = own_gram_ref[...]
    gram[1 - here % 2] = got_gram_ref[...]
    low_r = low_lanes(tall)
    low_l = low_lanes(2 * rows)

    @pl.loop(0, half, unroll=4)
    def _(chunk):
        weights = both[chunk]
        for p in range(0, pairs, 2):
            start = p % (pairs // 2) * 2 * rows
            found = jnp.dot(
                gram[p // (pairs // 2), start : start + 4 * rows + 16, :],
                weights,
                preferred_element_type=F32,
            )
            for side in range(2):
                block = 4 * chunk + 2 * side
                part = found[:, side * LANES : (side + 1) * LANES]
                for e in range(2):
                    first = part[2 * e * rows : 2 * e * rows + tall]
                    second = part[(2 * e + 1) * rows : (2 * e + 1) * rows + tall]
                    lanes = slice((p + e) * LANES, (p + e + 1) * LANES)
                    right[block, :, lanes] = jnp.where(low_r, first, pltpu.roll(second, BLK, 1)).astype(BF)
                    right[block + 1, :, lanes] = jnp.where(low_r, pltpu.roll(first, BLK, 1), second).astype(BF)
                part = found[:, (side + 2) * LANES : (side + 3) * LANES]
                first, second = part[0 : 2 * rows], part[2 * rows : 4 * rows]
                lanes = slice(p * BLK, p * BLK + LANES)
                left[block, :, lanes] = jnp.where(low_l, first, pltpu.roll(second, BLK, 1)).astype(BF)
                left[block + 1, :, lanes] = jnp.where(low_l, pltpu.roll(first, BLK, 1), second).astype(BF)

    row_pos = lax.broadcasted_iota(jnp.int32, (BLK, LANES), 0)
    row_dish = row_pos % (BLK // 2) * 2 + row_pos // (BLK // 2)
    ahead = lax.broadcasted_iota(jnp.int32, (BLK, LANES), 1) % BLK - row_dish
    low = low_lanes(BLK // 2)

    def place(block):
        return 2 * relative_place(block >> 1, here) + (block & 1) if relative else block

    for copy in copies:
        copy.wait()

    @pl.loop(0, (n_live + unroll - 1) // unroll)
    def _(group):
        slot_ids, pairs_of, leasts = [], [], []
        for u in range(unroll):
            turn = group * unroll + u
            is_mine = turn < n_mine
            slot = jnp.minimum(jnp.where(is_mine, turn, kept + turn - n_mine), slots - 1)
            row = jnp.where(is_mine, mine_ref[slot], other_ref[slot])
            col = jnp.where(is_mine, mine_ref[slots + slot], other_ref[slots + slot])
            slot_ids.append(slot)
            pairs_of.append((place(row), place(col)))
            leasts.append(jnp.where(turn < n_live, jnp.where(row == col, 0, -BLK), BLK))
        for u, slot in enumerate(slot_ids):
            for c in range(BLK // 2):
                stage[u, c * channels : (c + 1) * channels, :] = vis[
                    slot, :, c * LANES : (c + 1) * LANES
                ].astype(F32)
        models = [
            jnp.dot(turned[a][:, 0:tall], right[b], preferred_element_type=F32) for a, b in pairs_of
        ]
        residuals = []
        for u, slot in enumerate(slot_ids):
            keep = ahead > leasts[u]
            residual = []
            for p in range(pairs):
                first = stage[u, pl.ds(2 * p, BLK // 2, stride=channels), :]
                second = stage[u, pl.ds(2 * p + 1, BLK // 2, stride=channels), :]
                seen = jnp.concatenate(
                    [
                        jnp.where(low, first, pltpu.roll(second, BLK, 1)),
                        jnp.where(low, pltpu.roll(first, BLK, 1), second),
                    ],
                    0,
                )
                difference = models[u][:, p * LANES : (p + 1) * LANES] - seen
                residual.append(jnp.where(keep, difference, 0.0).astype(BF))
            residuals.append(residual)
        to_rows = [
            lax.dot_general(jnp.concatenate(residual, 1), right[b], NT, preferred_element_type=F32)
            for (a, b), residual in zip(pairs_of, residuals)
        ]
        to_cols = [
            jnp.dot(left[a], jnp.concatenate(residual, 0), preferred_element_type=F32)
            for (a, b), residual in zip(pairs_of, residuals)
        ]
        for (a, b), to_row, to_col in zip(pairs_of, to_rows, to_cols):
            row_sum[a, :, 0:tall] += to_row
            col_sum[b] += to_col

    low_out = low_lanes(rows)
    for where in range(2 * half):
        buf, base = where // per_tile, where % per_tile * LANES
        for side in range(2):
            total = row_sum[2 * where + side]
            start = base + side * BLK
            stage[buf, pl.ds(start, BLK // 2, stride=2), :] = total[0 : BLK // 2]
            stage[buf, pl.ds(start + 1, BLK // 2, stride=2), :] = total[BLK // 2 :]
    for where in range(2 * half):
        buf, base = where // per_tile, where % per_tile * LANES
        from_rows = stage[buf, base : base + LANES, :].T[0:rows]
        cols = []
        for side in range(2):
            total = col_sum[2 * where + side]
            cols.append(total[0:rows] + pltpu.roll(total[rows:], BLK, 1))
        from_cols = jnp.where(low_out, cols[0], pltpu.roll(cols[1], BLK, 1))
        result = ((from_rows + from_cols) * scale)[0:terms]
        if where < half:
            keep_ref[where] = result
        else:
            send_ref[where - half] = result


def tile_terms(relative, scale, mine, other, own, got, own_gram, got_gram, observed, more):
    slots, channels, _ = observed.shape
    half, terms, _ = own.shape
    rows, tall = up(terms, 8), up(terms, 16)
    blocks = 4 * half
    unroll = UNROLL
    smem = pl.BlockSpec(memory_space=pltpu.SMEM)
    vmem = pl.BlockSpec(memory_space=pltpu.VMEM)
    out = jax.ShapeDtypeStruct((half, terms, LANES), F32)
    return pl.pallas_call(
        functools.partial(tiles_kernel, relative, unroll, scale),
        out_shape=(out, out),
        in_specs=[smem, smem, vmem, vmem] + [pl.BlockSpec(memory_space=pl.ANY)] * 2 + [vmem] * 2,
        out_specs=(vmem, vmem),
        scratch_shapes=[
            pltpu.VMEM((slots, channels, BLK * BLK), BF),
            pltpu.VMEM((up(max(unroll, 2 * half * LANES // (channels * BLK // 2)), 1), channels * BLK // 2, LANES), F32),
            pltpu.VMEM((2 * half, LANES, LANES), F32),
            pltpu.VMEM((half, 2 * LANES, 4 * LANES), BF),
            pltpu.VMEM((2,) + own_gram.shape, BF),
            pltpu.VMEM((blocks, BLK, LANES), BF),
            pltpu.VMEM((blocks, tall, channels * BLK), BF),
            pltpu.VMEM((blocks, 2 * rows, channels // 2 * BLK), BF),
            pltpu.VMEM((blocks, BLK, LANES), F32),
            pltpu.VMEM((blocks, 2 * rows, LANES), F32),
            pltpu.SemaphoreType.DMA((2,)),
        ],
        compiler_params=pltpu.CompilerParams(vmem_limit_bytes=48 << 20),
        cost_estimate=pl.CostEstimate(
            flops=6 * slots * channels * BLK * BLK * terms, bytes_accessed=observed.size * 2, transcendentals=0
        ),
    )(mine, other, own, got, observed, more, own_gram, got_gram)


def from_partner(array, mask):
    return lax.ppermute(array, "tile", [(i, i ^ mask) for i in range(lax.axis_size("tile"))])


def on_device(
    coefficients, zernike_table, positions, source_flux, observed, tile_rows, tile_cols, tile_count
):
    members = lax.axis_size("tile")
    terms, shard = coefficients.shape
    dishes = members * shard
    scale = 1.0 / math.sqrt(dishes * positions.shape[0])
    channels, slots = positions.shape[0], tile_rows.shape[0]
    moved = slots // 4 + 1
    mine = jnp.concatenate([tile_rows, tile_cols, tile_count])
    to_move = observed[slots - moved :]
    own_gram = gram_of(zernike_table, positions, source_flux)
    if shard == LANES and members == 16:
        held = coefficients[None]
        held = jnp.concatenate([held, from_partner(held, 8)], 0)
        held, to_move, mine = lax.optimization_barrier((held, to_move, mine))
        more, other = from_partner(to_move, 1), from_partner(mine, 1)
        got_gram = from_partner(own_gram, 1)
        held = jnp.concatenate([held] + [from_partner(held, mask) for mask in (2, 4, 6)], 0)
        held, got_gram, other = lax.optimization_barrier((held, got_gram, other))
        got = from_partner(held, 1)
        total, sent = tile_terms(
            True, scale, mine, other, held, got, own_gram, got_gram, observed, more
        )
        total = total + from_partner(sent, 1)
        total = sum(
            [from_partner(total[mask : mask + 2], mask) for mask in (2, 4, 6)], total[:2]
        )
        total = total[:1] + from_partner(total[1:], 8)
        return total[0]
    more, other, got_gram = (from_partner(array, 1) for array in (to_move, mine, own_gram))
    everything = lax.all_gather(coefficients, "tile", axis=1, tiled=True)
    everything = everything.reshape(terms, dishes // LANES, LANES).transpose(1, 0, 2)
    half = everything.shape[0] // 2
    parts = tile_terms(
        False, scale, mine, other, everything[:half], everything[half:], own_gram, got_gram, observed, more
    )
    total = jnp.concatenate(parts, 0).transpose(1, 0, 2).reshape(terms, dishes)
    return lax.psum_scatter(total, "tile", scatter_dimension=1, tiled=True)


def solution(mesh):
    return jax.shard_map(
        on_device,
        mesh=mesh,
        in_specs=(
            P(None, "tile"),
            P(),
            P("scan", None),
            P("scan", None),
            P(("scan", "tile"), None, None),
            P(("scan", "tile")),
            P(("scan", "tile")),
            P(("scan", "tile")),
        ),
        out_specs=P("scan", "tile"),
        check_vma=False,
    )
```

```python
import functools
import math

import jax
import jax.numpy as jnp
from jax import lax
from jax.experimental import pallas as pl
from jax.experimental.pallas import tpu as pltpu
from jax.sharding import PartitionSpec as P

BLK = 64
UNROLL = 7
LANES = 128
PIXELS = 256
BF = jnp.bfloat16
F32 = jnp.float32
NT = (((1,), (1,)), ((), ()))


def up(size, unit):
    return -(-size // unit) * unit


def low_lanes(rows):
    return lax.broadcasted_iota(jnp.int32, (rows, LANES), 1) < BLK


def gram_kernel(root, table_ref, pos_ref, flux_ref, out_ref, groups, gram):
    terms, pixels = table_ref.shape
    channels, sources = pos_ref.shape
    count = channels // 2
    start = lax.axis_index("tile") % 2 * count
    n_groups = pixels // PIXELS
    tall = groups.shape[0] // n_groups
    rows = up(terms, 8)
    groups[...] = jnp.zeros_like(groups)
    gram[...] = jnp.zeros_like(gram)
    for h in range(n_groups):
        groups[h * tall : h * tall + terms, :] = table_ref[:, h * PIXELS : (h + 1) * PIXELS]
    pixel = lax.broadcasted_iota(jnp.int32, (PIXELS, sources), 0)
    for f in range(0, count, count):
        positions = [pos_ref[pl.ds(start + f + e, 1), :] for e in range(count)]
        hot = jnp.concatenate(
            [jnp.where(pixel == pos % PIXELS, 1.0, 0.0).astype(BF) for pos in positions], 1
        )
        found = jnp.dot(groups[...], hot, preferred_element_type=F32)
        for e, pos in enumerate(positions):
            group = pos // PIXELS
            chosen = jnp.zeros((tall, sources), F32)
            for h in range(n_groups):
                part = found[h * tall : (h + 1) * tall, e * sources : (e + 1) * sources]
                chosen = jnp.where(group == h, part, chosen)
            scaled = chosen * (flux_ref[pl.ds(start + f + e, 1), :] / root)
            high = scaled.astype(BF)
            low = (scaled - high.astype(F32)).astype(BF)
            chosen = chosen.astype(BF)
            product = lax.dot_general(high, chosen, NT, preferred_element_type=F32)
            product = product + lax.dot_general(low, chosen, NT, preferred_element_type=F32)
            gram[(f + e) * rows : (f + e) * rows + tall, 0:tall] = product
    value = gram[...]
    high = value.astype(BF)
    out_ref[:, 0:LANES] = high
    out_ref[:, LANES : 2 * LANES] = (value - high.astype(F32)).astype(BF)


def gram_of(zernike_table, positions, source_flux):
    terms, pixels = zernike_table.shape
    channels, sources = positions.shape
    count = channels // 2
    rows, tall = up(terms, 8), up(terms, 16)
    height = up(count * rows + 8, 16)
    return pl.pallas_call(
        functools.partial(gram_kernel, math.sqrt(sources)),
        out_shape=jax.ShapeDtypeStruct((height, 2 * LANES), BF),
        in_specs=[pl.BlockSpec(memory_space=pltpu.VMEM)] * 3,
        out_specs=pl.BlockSpec(memory_space=pltpu.VMEM),
        scratch_shapes=[
            pltpu.VMEM((pixels // PIXELS * tall, PIXELS), BF),
            pltpu.VMEM((height, LANES), F32),
        ],
        compiler_params=pltpu.CompilerParams(vmem_limit_bytes=32 << 20),
        cost_estimate=pl.CostEstimate(
            flops=2 * count * sources * pixels * terms, bytes_accessed=1 << 20, transcendentals=0
        ),
    )(zernike_table, positions, source_flux)


def relative_place(device, here):
    apart = device ^ here
    return 8 * (apart & 1) + (apart & 6) + (apart >> 3)


def tiles_kernel(
    relative, unroll, scale,
    mine_ref, other_ref, own_ref, got_ref, vis_hbm, more_hbm, own_gram_ref, got_gram_ref,
    keep_ref, send_ref,
    vis, stage, spread, both, gram, turned, right, left, row_sum, col_sum, sems,
):
    slots, channels = vis.shape[0], vis.shape[1]
    kept = slots - more_hbm.shape[0]
    half, terms = own_ref.shape[0], own_ref.shape[1]
    pairs = channels // 2
    rows, tall = up(terms, 8), up(terms, 16)
    n_mine = jnp.minimum(mine_ref[2 * slots], kept)
    n_live = n_mine + jnp.maximum(other_ref[2 * slots] - kept, 0)
    copies = (
        pltpu.make_async_copy(vis_hbm.at[pl.ds(0, kept)], vis.at[pl.ds(0, kept)], sems.at[0]),
        pltpu.make_async_copy(more_hbm, vis.at[pl.ds(kept, slots - kept)], sems.at[1]),
    )
    for copy in copies:
        copy.start()

    row_sum[...] = jnp.zeros_like(row_sum)
    col_sum[...] = jnp.zeros_like(col_sum)
    both[...] = jnp.zeros_like(both)
    per_tile = stage.shape[1] // LANES
    spread[...] = jnp.zeros_like(spread)

    for part, ref in enumerate((own_ref, got_ref)):
        for r in range(half):
            where = part * half + r
            chunk, lanes = where // 2, slice(where % 2 * LANES, (where % 2 + 1) * LANES)
            block = ref[r]
            both[chunk, 0:terms, lanes] = block
            both[chunk, LANES : LANES + terms, lanes] = block
            spread[where, 0:terms, :] = block.astype(F32)
            buf, base = where // per_tile, where % per_tile * LANES
            stage[buf, base : base + LANES, :] = spread[where].T
            sorted_rows = jnp.concatenate(
                [
                    stage[buf, pl.ds(base + start, BLK // 2, stride=2), :]
                    for start in (0, 1, BLK, BLK + 1)
                ],
                0,
            )
            turned[2 * where] = sorted_rows[0:BLK].astype(BF)
            turned[2 * where + 1] = sorted_rows[BLK:].astype(BF)
            back = sorted_rows.T.astype(BF)
            lanes = slice((where % 2 + 2) * LANES, (where % 2 + 3) * LANES)
            both[chunk, 0:LANES, lanes] = back
            both[chunk, LANES:, lanes] = back

    here = lax.axis_index("tile")
    gram[here % 2] = own_gram_ref[...]
    gram[1 - here % 2] = got_gram_ref[...]
    low_r = low_lanes(tall)
    low_l = low_lanes(2 * rows)

    @pl.loop(0, half, unroll=4)
    def _(chunk):
        weights = both[chunk]
        for p in range(0, pairs, 2):
            start = p % (pairs // 2) * 2 * rows
            found = jnp.dot(
                gram[p // (pairs // 2), start : start + 4 * rows + 16, :],
                weights,
                preferred_element_type=F32,
            )
            for side in range(2):
                block = 4 * chunk + 2 * side
                part = found[:, side * LANES : (side + 1) * LANES]
                for e in range(2):
                    first = part[2 * e * rows : 2 * e * rows + tall]
                    second = part[(2 * e + 1) * rows : (2 * e + 1) * rows + tall]
                    lanes = slice((p + e) * LANES, (p + e + 1) * LANES)
                    right[block, :, lanes] = jnp.where(low_r, first, pltpu.roll(second, BLK, 1)).astype(BF)
                    right[block + 1, :, lanes] = jnp.where(low_r, pltpu.roll(first, BLK, 1), second).astype(BF)
                part = found[:, (side + 2) * LANES : (side + 3) * LANES]
                first, second = part[0 : 2 * rows], part[2 * rows : 4 * rows]
                lanes = slice(p * BLK, p * BLK + LANES)
                left[block, :, lanes] = jnp.where(low_l, first, pltpu.roll(second, BLK, 1)).astype(BF)
                left[block + 1, :, lanes] = jnp.where(low_l, pltpu.roll(first, BLK, 1), second).astype(BF)

    row_pos = lax.broadcasted_iota(jnp.int32, (BLK, LANES), 0)
    row_dish = row_pos % (BLK // 2) * 2 + row_pos // (BLK // 2)
    ahead = lax.broadcasted_iota(jnp.int32, (BLK, LANES), 1) % BLK - row_dish
    low = low_lanes(BLK // 2)

    def place(block):
        return 2 * relative_place(block >> 1, here) + (block & 1) if relative else block

    for copy in copies:
        copy.wait()

    @pl.loop(0, (n_live + unroll - 1) // unroll)
    def _(group):
        slot_ids, pairs_of, leasts = [], [], []
        for u in range(unroll):
            turn = group * unroll + u
            is_mine = turn < n_mine
            slot = jnp.minimum(jnp.where(is_mine, turn, kept + turn - n_mine), slots - 1)
            row = jnp.where(is_mine, mine_ref[slot], other_ref[slot])
            col = jnp.where(is_mine, mine_ref[slots + slot], other_ref[slots + slot])
            slot_ids.append(slot)
            pairs_of.append((place(row), place(col)))
            leasts.append(jnp.where(turn < n_live, jnp.where(row == col, 0, -BLK), BLK))
        for u, slot in enumerate(slot_ids):
            for c in range(BLK // 2):
                stage[u, c * channels : (c + 1) * channels, :] = vis[
                    slot, :, c * LANES : (c + 1) * LANES
                ].astype(F32)
        models = [
            jnp.dot(turned[a][:, 0:tall], right[b], preferred_element_type=F32) for a, b in pairs_of
        ]
        residuals = []
        for u, slot in enumerate(slot_ids):
            keep = ahead > leasts[u]
            residual = []
            for p in range(pairs):
                first = stage[u, pl.ds(2 * p, BLK // 2, stride=channels), :]
                second = stage[u, pl.ds(2 * p + 1, BLK // 2, stride=channels), :]
                seen = jnp.concatenate(
                    [
                        jnp.where(low, first, pltpu.roll(second, BLK, 1)),
                        jnp.where(low, pltpu.roll(first, BLK, 1), second),
                    ],
                    0,
                )
                difference = models[u][:, p * LANES : (p + 1) * LANES] - seen
                residual.append(jnp.where(keep, difference, 0.0).astype(BF))
            residuals.append(residual)
        to_rows = [
            lax.dot_general(jnp.concatenate(residual, 1), right[b], NT, preferred_element_type=F32)
            for (a, b), residual in zip(pairs_of, residuals)
        ]
        to_cols = [
            jnp.dot(left[a], jnp.concatenate(residual, 0), preferred_element_type=F32)
            for (a, b), residual in zip(pairs_of, residuals)
        ]
        for (a, b), to_row, to_col in zip(pairs_of, to_rows, to_cols):
            row_sum[a, :, 0:tall] += to_row
            col_sum[b] += to_col

    low_out = low_lanes(rows)
    for where in range(2 * half):
        buf, base = where // per_tile, where % per_tile * LANES
        for side in range(2):
            total = row_sum[2 * where + side]
            start = base + side * BLK
            stage[buf, pl.ds(start, BLK // 2, stride=2), :] = total[0 : BLK // 2]
            stage[buf, pl.ds(start + 1, BLK // 2, stride=2), :] = total[BLK // 2 :]
    for where in range(2 * half):
        buf, base = where // per_tile, where % per_tile * LANES
        from_rows = stage[buf, base : base + LANES, :].T[0:rows]
        cols = []
        for side in range(2):
            total = col_sum[2 * where + side]
            cols.append(total[0:rows] + pltpu.roll(total[rows:], BLK, 1))
        from_cols = jnp.where(low_out, cols[0], pltpu.roll(cols[1], BLK, 1))
        result = ((from_rows + from_cols) * scale)[0:terms]
        if where < half:
            keep_ref[where] = result
        else:
            send_ref[where - half] = result


def tile_terms(relative, scale, mine, other, own, got, own_gram, got_gram, observed, more):
    slots, channels, _ = observed.shape
    half, terms, _ = own.shape
    rows, tall = up(terms, 8), up(terms, 16)
    blocks = 4 * half
    unroll = UNROLL
    smem = pl.BlockSpec(memory_space=pltpu.SMEM)
    vmem = pl.BlockSpec(memory_space=pltpu.VMEM)
    out = jax.ShapeDtypeStruct((half, terms, LANES), F32)
    return pl.pallas_call(
        functools.partial(tiles_kernel, relative, unroll, scale),
        out_shape=(out, out),
        in_specs=[smem, smem, vmem, vmem] + [pl.BlockSpec(memory_space=pl.ANY)] * 2 + [vmem] * 2,
        out_specs=(vmem, vmem),
        scratch_shapes=[
            pltpu.VMEM((slots, channels, BLK * BLK), BF),
            pltpu.VMEM((up(max(unroll, 2 * half * LANES // (channels * BLK // 2)), 1), channels * BLK // 2, LANES), F32),
            pltpu.VMEM((2 * half, LANES, LANES), F32),
            pltpu.VMEM((half, 2 * LANES, 4 * LANES), BF),
            pltpu.VMEM((2,) + own_gram.shape, BF),
            pltpu.VMEM((blocks, BLK, LANES), BF),
            pltpu.VMEM((blocks, tall, channels * BLK), BF),
            pltpu.VMEM((blocks, 2 * rows, channels // 2 * BLK), BF),
            pltpu.VMEM((blocks, BLK, LANES), F32),
            pltpu.VMEM((blocks, 2 * rows, LANES), F32),
            pltpu.SemaphoreType.DMA((2,)),
        ],
        compiler_params=pltpu.CompilerParams(vmem_limit_bytes=48 << 20),
        cost_estimate=pl.CostEstimate(
            flops=6 * slots * channels * BLK * BLK * terms, bytes_accessed=observed.size * 2, transcendentals=0
        ),
    )(mine, other, own, got, observed, more, own_gram, got_gram)


def from_partner(array, mask):
    return lax.ppermute(array, "tile", [(i, i ^ mask) for i in range(lax.axis_size("tile"))])


def on_device(
    coefficients, zernike_table, positions, source_flux, observed, tile_rows, tile_cols, tile_count
):
    members = lax.axis_size("tile")
    terms, shard = coefficients.shape
    dishes = members * shard
    scale = 1.0 / math.sqrt(dishes * positions.shape[0])
    channels, slots = positions.shape[0], tile_rows.shape[0]
    moved = slots // 4 + 1
    mine = jnp.concatenate([tile_rows, tile_cols, tile_count])
    to_move = observed[slots - moved :]
    own_gram = gram_of(zernike_table, positions, source_flux)
    if shard == LANES and members == 16:
        held = coefficients[None]
        held = jnp.concatenate([held, from_partner(held, 8)], 0)
        held, own_gram = lax.optimization_barrier((held, own_gram))
        more, other = from_partner(to_move, 1), from_partner(mine, 1)
        got_gram = from_partner(own_gram, 1)
        held = jnp.concatenate([held] + [from_partner(held, mask) for mask in (2, 4, 6)], 0)
        held, got_gram, other = lax.optimization_barrier((held, got_gram, other))
        got = from_partner(held, 1)
        total, sent = tile_terms(
            True, scale, mine, other, held, got, own_gram, got_gram, observed, more
        )
        total = total + from_partner(sent, 1)
        total = sum(
            [from_partner(total[mask : mask + 2], mask) for mask in (2, 4, 6)], total[:2]
        )
        total = total[:1] + from_partner(total[1:], 8)
        return total[0]
    more, other, got_gram = (from_partner(array, 1) for array in (to_move, mine, own_gram))
    everything = lax.all_gather(coefficients, "tile", axis=1, tiled=True)
    everything = everything.reshape(terms, dishes // LANES, LANES).transpose(1, 0, 2)
    half = everything.shape[0] // 2
    parts = tile_terms(
        False, scale, mine, other, everything[:half], everything[half:], own_gram, got_gram, observed, more
    )
    total = jnp.concatenate(parts, 0).transpose(1, 0, 2).reshape(terms, dishes)
    return lax.psum_scatter(total, "tile", scatter_dimension=1, tiled=True)


def solution(mesh):
    return jax.shard_map(
        on_device,
        mesh=mesh,
        in_specs=(
            P(None, "tile"),
            P(),
            P("scan", None),
            P("scan", None),
            P(("scan", "tile"), None, None),
            P(("scan", "tile")),
            P(("scan", "tile")),
            P(("scan", "tile")),
        ),
        out_specs=P("scan", "tile"),
        check_vma=False,
    )
```

```python
import functools
import math

import jax
import jax.numpy as jnp
from jax import lax
from jax.experimental import pallas as pl
from jax.experimental.pallas import tpu as pltpu
from jax.sharding import PartitionSpec as P

BLK = 64
PITCH = 18
UNROLL = 7
LANES = 128
PIXELS = 256
BF = jnp.bfloat16
F32 = jnp.float32
NT = (((1,), (1,)), ((), ()))


def up(size, unit):
    return -(-size // unit) * unit


def low_lanes(rows):
    return lax.broadcasted_iota(jnp.int32, (rows, LANES), 1) < BLK


def gram_kernel(root, table_ref, pos_ref, flux_ref, out_ref, groups, gram):
    terms, pixels = table_ref.shape
    channels, sources = pos_ref.shape
    count = channels // 2
    start = lax.axis_index("tile") % 2 * count
    n_groups = pixels // PIXELS
    tall = groups.shape[0] // n_groups
    rows = up(terms, 8)
    groups[...] = jnp.zeros_like(groups)
    gram[...] = jnp.zeros_like(gram)
    for h in range(n_groups):
        groups[h * tall : h * tall + terms, :] = table_ref[:, h * PIXELS : (h + 1) * PIXELS]
    pixel = lax.broadcasted_iota(jnp.int32, (PIXELS, sources), 0)
    for f in range(0, count, count):
        positions = [pos_ref[pl.ds(start + f + e, 1), :] for e in range(count)]
        hot = jnp.concatenate(
            [jnp.where(pixel == pos % PIXELS, 1.0, 0.0).astype(BF) for pos in positions], 1
        )
        found = jnp.dot(groups[...], hot, preferred_element_type=F32)
        for e, pos in enumerate(positions):
            group = pos // PIXELS
            chosen = jnp.zeros((tall, sources), F32)
            for h in range(n_groups):
                part = found[h * tall : (h + 1) * tall, e * sources : (e + 1) * sources]
                chosen = jnp.where(group == h, part, chosen)
            scaled = chosen * (flux_ref[pl.ds(start + f + e, 1), :] / root)
            high = scaled.astype(BF)
            low = (scaled - high.astype(F32)).astype(BF)
            chosen = chosen.astype(BF)
            product = lax.dot_general(high, chosen, NT, preferred_element_type=F32)
            product = product + lax.dot_general(low, chosen, NT, preferred_element_type=F32)
            gram[(f + e) * rows : (f + e) * rows + tall, 0:tall] = product
    value = gram[...]
    high = value.astype(BF)
    out_ref[:, 0:LANES] = high
    out_ref[:, LANES : 2 * LANES] = (value - high.astype(F32)).astype(BF)


def gram_of(zernike_table, positions, source_flux):
    terms, pixels = zernike_table.shape
    channels, sources = positions.shape
    count = channels // 2
    rows, tall = up(terms, 8), up(terms, 16)
    height = up(count * rows + 8, 16)
    return pl.pallas_call(
        functools.partial(gram_kernel, math.sqrt(sources)),
        out_shape=jax.ShapeDtypeStruct((height, 2 * LANES), BF),
        in_specs=[pl.BlockSpec(memory_space=pltpu.VMEM)] * 3,
        out_specs=pl.BlockSpec(memory_space=pltpu.VMEM),
        scratch_shapes=[
            pltpu.VMEM((pixels // PIXELS * tall, PIXELS), BF),
            pltpu.VMEM((height, LANES), F32),
        ],
        compiler_params=pltpu.CompilerParams(vmem_limit_bytes=32 << 20),
        cost_estimate=pl.CostEstimate(
            flops=2 * count * sources * pixels * terms, bytes_accessed=1 << 20, transcendentals=0
        ),
    )(zernike_table, positions, source_flux)


def relative_place(device, here):
    apart = device ^ here
    return 8 * (apart & 1) + (apart & 6) + (apart >> 3)


def tiles_kernel(
    relative, unroll, scale,
    mine_ref, other_ref, own_ref, got_ref, vis_hbm, more_hbm, own_gram_ref, got_gram_ref,
    keep_ref, send_ref,
    vis, stage, spread, both, gram, turned, right, left, row_sum, col_sum, sems,
):
    slots, channels = vis.shape[0], vis.shape[1]
    kept = slots - more_hbm.shape[0]
    half, terms = own_ref.shape[0], own_ref.shape[1]
    pairs = channels // 2
    rows, tall = up(terms, 8), up(terms, 16)
    n_mine = jnp.minimum(mine_ref[2 * slots], kept)
    n_live = n_mine + jnp.maximum(other_ref[2 * slots] - kept, 0)
    copies = (
        pltpu.make_async_copy(vis_hbm.at[pl.ds(0, kept)], vis.at[pl.ds(0, kept)], sems.at[0]),
        pltpu.make_async_copy(more_hbm, vis.at[pl.ds(kept, slots - kept)], sems.at[1]),
    )
    for copy in copies:
        copy.start()

    row_sum[...] = jnp.zeros_like(row_sum)
    col_sum[...] = jnp.zeros_like(col_sum)
    both[...] = jnp.zeros_like(both)
    per_tile = stage.shape[1] // LANES
    spread[...] = jnp.zeros_like(spread)

    for part, ref in enumerate((own_ref, got_ref)):
        for r in range(half):
            where = part * half + r
            chunk, lanes = where // 2, slice(where % 2 * LANES, (where % 2 + 1) * LANES)
            block = ref[r]
            both[chunk, 0:terms, lanes] = block
            both[chunk, LANES : LANES + terms, lanes] = block
            spread[where, 0:terms, :] = block.astype(F32)
            buf, base = where // per_tile, where % per_tile * LANES
            stage[buf, base : base + LANES, :] = spread[where].T
            sorted_rows = jnp.concatenate(
                [
                    stage[buf, pl.ds(base + start, BLK // 2, stride=2), :]
                    for start in (0, 1, BLK, BLK + 1)
                ],
                0,
            )
            turned[2 * where] = sorted_rows[0:BLK].astype(BF)
            turned[2 * where + 1] = sorted_rows[BLK:].astype(BF)
            back = sorted_rows.T.astype(BF)
            lanes = slice((where % 2 + 2) * LANES, (where % 2 + 3) * LANES)
            both[chunk, 0:LANES, lanes] = back
            both[chunk, LANES:, lanes] = back

    here = lax.axis_index("tile")
    gram[here % 2] = own_gram_ref[...]
    gram[1 - here % 2] = got_gram_ref[...]
    low_r = low_lanes(tall)
    low_l = low_lanes(2 * rows)

    @pl.loop(0, half, unroll=4)
    def _(chunk):
        weights = both[chunk]
        for p in range(0, pairs, 2):
            start = p % (pairs // 2) * 2 * rows
            found = jnp.dot(
                gram[p // (pairs // 2), start : start + 4 * rows + 16, :],
                weights,
                preferred_element_type=F32,
            )
            for side in range(2):
                block = 4 * chunk + 2 * side
                part = found[:, side * LANES : (side + 1) * LANES]
                for e in range(2):
                    first = part[2 * e * rows : 2 * e * rows + tall]
                    second = part[(2 * e + 1) * rows : (2 * e + 1) * rows + tall]
                    lanes = slice((p + e) * LANES, (p + e + 1) * LANES)
                    right[block, :, lanes] = jnp.where(low_r, first, pltpu.roll(second, BLK, 1)).astype(BF)
                    right[block + 1, :, lanes] = jnp.where(low_r, pltpu.roll(first, BLK, 1), second).astype(BF)
                part = found[:, (side + 2) * LANES : (side + 3) * LANES]
                first, second = part[0 : 2 * rows], part[2 * rows : 4 * rows]
                lanes = slice(p * BLK, p * BLK + LANES)
                left[block, :, lanes] = jnp.where(low_l, first, pltpu.roll(second, BLK, 1)).astype(BF)
                left[block + 1, :, lanes] = jnp.where(low_l, pltpu.roll(first, BLK, 1), second).astype(BF)

    row_pos = lax.broadcasted_iota(jnp.int32, (BLK, LANES), 0)
    row_dish = row_pos % (BLK // 2) * 2 + row_pos // (BLK // 2)
    ahead = lax.broadcasted_iota(jnp.int32, (BLK, LANES), 1) % BLK - row_dish
    low = low_lanes(BLK // 2)

    def place(block):
        return 2 * relative_place(block >> 1, here) + (block & 1) if relative else block

    for copy in copies:
        copy.wait()

    @pl.loop(0, (n_live + unroll - 1) // unroll)
    def _(group):
        slot_ids, pairs_of, leasts = [], [], []
        for u in range(unroll):
            turn = group * unroll + u
            is_mine = turn < n_mine
            slot = jnp.minimum(jnp.where(is_mine, turn, kept + turn - n_mine), slots - 1)
            row = jnp.where(is_mine, mine_ref[slot], other_ref[slot])
            col = jnp.where(is_mine, mine_ref[slots + slot], other_ref[slots + slot])
            slot_ids.append(slot)
            pairs_of.append((place(row), place(col)))
            leasts.append(jnp.where(turn < n_live, jnp.where(row == col, 0, -BLK), BLK))
        for u, slot in enumerate(slot_ids):
            for c in range(BLK // 2):
                stage[u, c * PITCH : c * PITCH + channels, :] = vis[
                    slot, :, c * LANES : (c + 1) * LANES
                ].astype(F32)
        models = [
            jnp.dot(turned[a][:, 0:tall], right[b], preferred_element_type=F32) for a, b in pairs_of
        ]
        residuals = []
        for u, slot in enumerate(slot_ids):
            keep = ahead > leasts[u]
            residual = []
            for p in range(pairs):
                first = stage[u, pl.ds(2 * p, BLK // 2, stride=PITCH), :]
                second = stage[u, pl.ds(2 * p + 1, BLK // 2, stride=PITCH), :]
                first, second = first.astype(BF), second.astype(BF)
                seen = jnp.concatenate(
                    [
                        jnp.concatenate([first[:, :BLK], second[:, :BLK]], 1),
                        jnp.concatenate([first[:, BLK:], second[:, BLK:]], 1),
                    ],
                    0,
                ).astype(F32)
                difference = models[u][:, p * LANES : (p + 1) * LANES] - seen
                residual.append(jnp.where(keep, difference, 0.0).astype(BF))
            residuals.append(residual)
        to_rows = [
            lax.dot_general(jnp.concatenate(residual, 1), right[b], NT, preferred_element_type=F32)
            for (a, b), residual in zip(pairs_of, residuals)
        ]
        to_cols = [
            jnp.dot(left[a], jnp.concatenate(residual, 0), preferred_element_type=F32)
            for (a, b), residual in zip(pairs_of, residuals)
        ]
        for (a, b), to_row, to_col in zip(pairs_of, to_rows, to_cols):
            row_sum[a, :, 0:tall] += to_row
            col_sum[b] += to_col

    low_out = low_lanes(rows)
    for where in range(2 * half):
        buf, base = where // per_tile, where % per_tile * LANES
        for side in range(2):
            total = row_sum[2 * where + side]
            start = base + side * BLK
            stage[buf, pl.ds(start, BLK // 2, stride=2), :] = total[0 : BLK // 2]
            stage[buf, pl.ds(start + 1, BLK // 2, stride=2), :] = total[BLK // 2 :]
    for where in range(2 * half):
        buf, base = where // per_tile, where % per_tile * LANES
        from_rows = stage[buf, base : base + LANES, :].T[0:rows]
        cols = []
        for side in range(2):
            total = col_sum[2 * where + side]
            cols.append(total[0:rows] + pltpu.roll(total[rows:], BLK, 1))
        from_cols = jnp.where(low_out, cols[0], pltpu.roll(cols[1], BLK, 1))
        result = ((from_rows + from_cols) * scale)[0:terms]
        if where < half:
            keep_ref[where] = result
        else:
            send_ref[where - half] = result


def tile_terms(relative, scale, mine, other, own, got, own_gram, got_gram, observed, more):
    slots, channels, _ = observed.shape
    half, terms, _ = own.shape
    rows, tall = up(terms, 8), up(terms, 16)
    blocks = 4 * half
    unroll = UNROLL
    smem = pl.BlockSpec(memory_space=pltpu.SMEM)
    vmem = pl.BlockSpec(memory_space=pltpu.VMEM)
    out = jax.ShapeDtypeStruct((half, terms, LANES), F32)
    return pl.pallas_call(
        functools.partial(tiles_kernel, relative, unroll, scale),
        out_shape=(out, out),
        in_specs=[smem, smem, vmem, vmem] + [pl.BlockSpec(memory_space=pl.ANY)] * 2 + [vmem] * 2,
        out_specs=(vmem, vmem),
        scratch_shapes=[
            pltpu.VMEM((slots, channels, BLK * BLK), BF),
            pltpu.VMEM((max(unroll, -(-2 * half // (PITCH * BLK // 2 // LANES))), PITCH * BLK // 2, LANES), F32),
            pltpu.VMEM((2 * half, LANES, LANES), F32),
            pltpu.VMEM((half, 2 * LANES, 4 * LANES), BF),
            pltpu.VMEM((2,) + own_gram.shape, BF),
            pltpu.VMEM((blocks, BLK, LANES), BF),
            pltpu.VMEM((blocks, tall, channels * BLK), BF),
            pltpu.VMEM((blocks, 2 * rows, channels // 2 * BLK), BF),
            pltpu.VMEM((blocks, BLK, LANES), F32),
            pltpu.VMEM((blocks, 2 * rows, LANES), F32),
            pltpu.SemaphoreType.DMA((2,)),
        ],
        compiler_params=pltpu.CompilerParams(vmem_limit_bytes=48 << 20),
        cost_estimate=pl.CostEstimate(
            flops=6 * slots * channels * BLK * BLK * terms, bytes_accessed=observed.size * 2, transcendentals=0
        ),
    )(mine, other, own, got, observed, more, own_gram, got_gram)


def from_partner(array, mask):
    return lax.ppermute(array, "tile", [(i, i ^ mask) for i in range(lax.axis_size("tile"))])


def on_device(
    coefficients, zernike_table, positions, source_flux, observed, tile_rows, tile_cols, tile_count
):
    members = lax.axis_size("tile")
    terms, shard = coefficients.shape
    dishes = members * shard
    scale = 1.0 / math.sqrt(dishes * positions.shape[0])
    channels, slots = positions.shape[0], tile_rows.shape[0]
    moved = slots // 4 + 1
    mine = jnp.concatenate([tile_rows, tile_cols, tile_count])
    to_move = observed[slots - moved :]
    own_gram = gram_of(zernike_table, positions, source_flux)
    if shard == LANES and members == 16:
        held = coefficients[None]
        held = jnp.concatenate([held, from_partner(held, 8)], 0)
        held, own_gram = lax.optimization_barrier((held, own_gram))
        more, other = from_partner(to_move, 1), from_partner(mine, 1)
        got_gram = from_partner(own_gram, 1)
        held = jnp.concatenate([held] + [from_partner(held, mask) for mask in (6, 4, 2)][::-1], 0)
        held, got_gram, other = lax.optimization_barrier((held, got_gram, other))
        got = from_partner(held, 1)
        total, sent = tile_terms(
            True, scale, mine, other, held, got, own_gram, got_gram, observed, more
        )
        total = total + from_partner(sent, 1)
        total = sum(
            [from_partner(total[mask : mask + 2], mask) for mask in (6, 4, 2)], total[:2]
        )
        total = total[:1] + from_partner(total[1:], 8)
        return total[0]
    more, other, got_gram = (from_partner(array, 1) for array in (to_move, mine, own_gram))
    everything = lax.all_gather(coefficients, "tile", axis=1, tiled=True)
    everything = everything.reshape(terms, dishes // LANES, LANES).transpose(1, 0, 2)
    half = everything.shape[0] // 2
    parts = tile_terms(
        False, scale, mine, other, everything[:half], everything[half:], own_gram, got_gram, observed, more
    )
    total = jnp.concatenate(parts, 0).transpose(1, 0, 2).reshape(terms, dishes)
    return lax.psum_scatter(total, "tile", scatter_dimension=1, tiled=True)


def solution(mesh):
    return jax.shard_map(
        on_device,
        mesh=mesh,
        in_specs=(
            P(None, "tile"),
            P(),
            P("scan", None),
            P("scan", None),
            P(("scan", "tile"), None, None),
            P(("scan", "tile")),
            P(("scan", "tile")),
            P(("scan", "tile")),
        ),
        out_specs=P("scan", "tile"),
        check_vma=False,
    )
```

```python
import functools
import math

import jax
import jax.numpy as jnp
from jax import lax
from jax.experimental import pallas as pl
from jax.experimental.pallas import tpu as pltpu
from jax.sharding import PartitionSpec as P

BLK = 64
PITCH = 18
UNROLL = 7
LANES = 128
PIXELS = 256
BF = jnp.bfloat16
F32 = jnp.float32
NT = (((1,), (1,)), ((), ()))


def up(size, unit):
    return -(-size // unit) * unit


def sorting(size, transposed=False):
    natural = lax.broadcasted_iota(jnp.int32, (size, size), 1 if transposed else 0)
    place = lax.broadcasted_iota(jnp.int32, (size, size), 0 if transposed else 1)
    inside = place % BLK
    source = place - inside + inside % (BLK // 2) * 2 + inside // (BLK // 2)
    return jnp.where(natural == source, 1.0, 0.0).astype(BF)


def low_lanes(rows):
    return lax.broadcasted_iota(jnp.int32, (rows, LANES), 1) < BLK


def gram_kernel(root, table_ref, pos_ref, flux_ref, out_ref, groups, gram):
    terms, pixels = table_ref.shape
    channels, sources = pos_ref.shape
    count = channels // 2
    start = lax.axis_index("tile") % 2 * count
    n_groups = pixels // PIXELS
    tall = groups.shape[0] // n_groups
    rows = up(terms, 8)
    groups[...] = jnp.zeros_like(groups)
    gram[...] = jnp.zeros_like(gram)
    for h in range(n_groups):
        groups[h * tall : h * tall + terms, :] = table_ref[:, h * PIXELS : (h + 1) * PIXELS]
    pixel = lax.broadcasted_iota(jnp.int32, (PIXELS, sources), 0)
    for f in range(0, count, count):
        positions = [pos_ref[pl.ds(start + f + e, 1), :] for e in range(count)]
        hot = jnp.concatenate(
            [jnp.where(pixel == pos % PIXELS, 1.0, 0.0).astype(BF) for pos in positions], 1
        )
        found = jnp.dot(groups[...], hot, preferred_element_type=F32)
        for e, pos in enumerate(positions):
            group = pos // PIXELS
            chosen = jnp.zeros((tall, sources), F32)
            for h in range(n_groups):
                part = found[h * tall : (h + 1) * tall, e * sources : (e + 1) * sources]
                chosen = jnp.where(group == h, part, chosen)
            scaled = chosen * (flux_ref[pl.ds(start + f + e, 1), :] / root)
            high = scaled.astype(BF)
            low = (scaled - high.astype(F32)).astype(BF)
            chosen = chosen.astype(BF)
            product = lax.dot_general(high, chosen, NT, preferred_element_type=F32)
            product = product + lax.dot_general(low, chosen, NT, preferred_element_type=F32)
            gram[(f + e) * rows : (f + e) * rows + tall, 0:tall] = product
    value = gram[...]
    high = value.astype(BF)
    out_ref[:, 0:LANES] = high
    out_ref[:, LANES : 2 * LANES] = (value - high.astype(F32)).astype(BF)


def gram_of(zernike_table, positions, source_flux):
    terms, pixels = zernike_table.shape
    channels, sources = positions.shape
    count = channels // 2
    rows, tall = up(terms, 8), up(terms, 16)
    height = up(count * rows + 8, 16)
    return pl.pallas_call(
        functools.partial(gram_kernel, math.sqrt(sources)),
        out_shape=jax.ShapeDtypeStruct((height, 2 * LANES), BF),
        in_specs=[pl.BlockSpec(memory_space=pltpu.VMEM)] * 3,
        out_specs=pl.BlockSpec(memory_space=pltpu.VMEM),
        scratch_shapes=[
            pltpu.VMEM((pixels // PIXELS * tall, PIXELS), BF),
            pltpu.VMEM((height, LANES), F32),
        ],
        compiler_params=pltpu.CompilerParams(vmem_limit_bytes=32 << 20),
        cost_estimate=pl.CostEstimate(
            flops=2 * count * sources * pixels * terms, bytes_accessed=1 << 20, transcendentals=0
        ),
    )(zernike_table, positions, source_flux)


def relative_place(device, here):
    apart = device ^ here
    return 8 * (apart & 1) + (apart & 6) + (apart >> 3)


def tiles_kernel(
    relative, unroll, scale,
    mine_ref, other_ref, own_ref, got_ref, vis_hbm, more_hbm, own_gram_ref, got_gram_ref,
    keep_ref, send_ref,
    vis, stage, both, gram, turned, right, left, row_sum, col_sum, sems,
):
    slots, channels = vis.shape[0], vis.shape[1]
    kept = slots - more_hbm.shape[0]
    half, terms = own_ref.shape[0], own_ref.shape[1]
    pairs = channels // 2
    rows, tall = up(terms, 8), up(terms, 16)
    n_mine = jnp.minimum(mine_ref[2 * slots], kept)
    n_live = n_mine + jnp.maximum(other_ref[2 * slots] - kept, 0)
    copies = (
        pltpu.make_async_copy(vis_hbm.at[pl.ds(0, kept)], vis.at[pl.ds(0, kept)], sems.at[0]),
        pltpu.make_async_copy(more_hbm, vis.at[pl.ds(kept, slots - kept)], sems.at[1]),
    )
    for copy in copies:
        copy.start()

    row_sum[...] = jnp.zeros_like(row_sum)
    col_sum[...] = jnp.zeros_like(col_sum)
    both[...] = jnp.zeros_like(both)
    per_tile = stage.shape[1] // LANES

    for part, ref in enumerate((own_ref, got_ref)):
        for r in range(half):
            where = part * half + r
            chunk, lanes = where // 2, slice(where % 2 * LANES, (where % 2 + 1) * LANES)
            both[chunk, 0:terms, lanes] = ref[r]
            both[chunk, LANES : LANES + terms, lanes] = ref[r]
    order, order_of = sorting(2 * LANES), sorting(LANES, True)
    halves = jnp.concatenate([both[chunk, 0:LANES, 0 : 2 * LANES] for chunk in range(half)], 0)
    mixed = jnp.dot(halves, order, preferred_element_type=F32).astype(BF)
    for chunk in range(half):
        piece = mixed[chunk * LANES : (chunk + 1) * LANES]
        both[chunk, 0:LANES, 2 * LANES :] = piece
        both[chunk, LANES:, 2 * LANES :] = piece
    for chunk in range(half):
        for side in range(2):
            block = both[chunk, 0:LANES, side * LANES : (side + 1) * LANES]
            sorted_rows = lax.dot_general(order_of, block, NT, preferred_element_type=F32).astype(BF)
            turned[4 * chunk + 2 * side] = sorted_rows[0:BLK]
            turned[4 * chunk + 2 * side + 1] = sorted_rows[BLK:]

    here = lax.axis_index("tile")
    gram[here % 2] = own_gram_ref[...]
    gram[1 - here % 2] = got_gram_ref[...]
    low_r = low_lanes(tall)
    low_l = low_lanes(2 * rows)

    @pl.loop(0, half, unroll=8)
    def _(chunk):
        weights = both[chunk]
        for p in range(0, pairs, 2):
            start = p % (pairs // 2) * 2 * rows
            found = jnp.dot(
                gram[p // (pairs // 2), start : start + 4 * rows + 16, :],
                weights,
                preferred_element_type=F32,
            )
            for side in range(2):
                block = 4 * chunk + 2 * side
                part = found[:, side * LANES : (side + 1) * LANES]
                for e in range(2):
                    first = part[2 * e * rows : 2 * e * rows + tall]
                    second = part[(2 * e + 1) * rows : (2 * e + 1) * rows + tall]
                    lanes = slice((p + e) * LANES, (p + e + 1) * LANES)
                    first, second = first.astype(BF), second.astype(BF)
                    right[block, :, lanes] = jnp.concatenate([first[:, :BLK], second[:, :BLK]], 1)
                    right[block + 1, :, lanes] = jnp.concatenate([first[:, BLK:], second[:, BLK:]], 1)
                part = found[:, (side + 2) * LANES : (side + 3) * LANES]
                first, second = part[0 : 2 * rows], part[2 * rows : 4 * rows]
                lanes = slice(p * BLK, p * BLK + LANES)
                first, second = first.astype(BF), second.astype(BF)
                left[block, :, lanes] = jnp.concatenate([first[:, :BLK], second[:, :BLK]], 1)
                left[block + 1, :, lanes] = jnp.concatenate([first[:, BLK:], second[:, BLK:]], 1)

    row_pos = lax.broadcasted_iota(jnp.int32, (BLK, LANES), 0)
    row_dish = row_pos % (BLK // 2) * 2 + row_pos // (BLK // 2)
    ahead = lax.broadcasted_iota(jnp.int32, (BLK, LANES), 1) % BLK - row_dish
    low = low_lanes(BLK // 2)

    def place(block):
        return 2 * relative_place(block >> 1, here) + (block & 1) if relative else block

    for copy in copies:
        copy.wait()

    @pl.loop(0, (n_live + unroll - 1) // unroll)
    def _(group):
        slot_ids, pairs_of, leasts = [], [], []
        for u in range(unroll):
            turn = group * unroll + u
            is_mine = turn < n_mine
            slot = jnp.minimum(jnp.where(is_mine, turn, kept + turn - n_mine), slots - 1)
            row = jnp.where(is_mine, mine_ref[slot], other_ref[slot])
            col = jnp.where(is_mine, mine_ref[slots + slot], other_ref[slots + slot])
            slot_ids.append(slot)
            pairs_of.append((place(row), place(col)))
            leasts.append(jnp.where(turn < n_live, jnp.where(row == col, 0, -BLK), BLK))
        for u, slot in enumerate(slot_ids):
            for c in range(BLK // 2):
                stage[u, c * PITCH : c * PITCH + channels, :] = vis[
                    slot, :, c * LANES : (c + 1) * LANES
                ].astype(F32)
        models = [
            jnp.dot(turned[a][:, 0:tall], right[b], preferred_element_type=F32) for a, b in pairs_of
        ]
        residuals = []
        for u, slot in enumerate(slot_ids):
            keep = ahead > leasts[u]
            residual = []
            for p in range(pairs):
                first = stage[u, pl.ds(2 * p, BLK // 2, stride=PITCH), :]
                second = stage[u, pl.ds(2 * p + 1, BLK // 2, stride=PITCH), :]
                first, second = first.astype(BF), second.astype(BF)
                seen = jnp.concatenate(
                    [
                        jnp.concatenate([first[:, :BLK], second[:, :BLK]], 1),
                        jnp.concatenate([first[:, BLK:], second[:, BLK:]], 1),
                    ],
                    0,
                ).astype(F32)
                difference = models[u][:, p * LANES : (p + 1) * LANES] - seen
                residual.append(jnp.where(keep, difference, 0.0).astype(BF))
            residuals.append(residual)
        to_rows = [
            lax.dot_general(jnp.concatenate(residual, 1), right[b], NT, preferred_element_type=F32)
            for (a, b), residual in zip(pairs_of, residuals)
        ]
        to_cols = [
            jnp.dot(left[a], jnp.concatenate(residual, 0), preferred_element_type=F32)
            for (a, b), residual in zip(pairs_of, residuals)
        ]
        for (a, b), to_row, to_col in zip(pairs_of, to_rows, to_cols):
            row_sum[a, :, 0:tall] += to_row
            col_sum[b] += to_col

    low_out = low_lanes(rows)
    for where in range(2 * half):
        buf, base = where // per_tile, where % per_tile * LANES
        for side in range(2):
            total = row_sum[2 * where + side]
            start = base + side * BLK
            stage[buf, pl.ds(start, BLK // 2, stride=2), :] = total[0 : BLK // 2]
            stage[buf, pl.ds(start + 1, BLK // 2, stride=2), :] = total[BLK // 2 :]
    for where in range(2 * half):
        buf, base = where // per_tile, where % per_tile * LANES
        from_rows = stage[buf, base : base + LANES, :].T[0:rows]
        first, second = col_sum[2 * where], col_sum[2 * where + 1]
        straight = jnp.where(low_out, first[0:rows], second[rows:])
        crossed = jnp.where(low_out, second[0:rows], first[rows:])
        from_cols = straight + pltpu.roll(crossed, BLK, 1)
        result = ((from_rows + from_cols) * scale)[0:terms]
        if where < half:
            keep_ref[where] = result
        else:
            send_ref[where - half] = result


def tile_terms(relative, scale, mine, other, own, got, own_gram, got_gram, observed, more):
    slots, channels, _ = observed.shape
    half, terms, _ = own.shape
    rows, tall = up(terms, 8), up(terms, 16)
    blocks = 4 * half
    unroll = UNROLL
    smem = pl.BlockSpec(memory_space=pltpu.SMEM)
    vmem = pl.BlockSpec(memory_space=pltpu.VMEM)
    out = jax.ShapeDtypeStruct((half, terms, LANES), F32)
    return pl.pallas_call(
        functools.partial(tiles_kernel, relative, unroll, scale),
        out_shape=(out, out),
        in_specs=[smem, smem, vmem, vmem] + [pl.BlockSpec(memory_space=pl.ANY)] * 2 + [vmem] * 2,
        out_specs=(vmem, vmem),
        scratch_shapes=[
            pltpu.VMEM((slots, channels, BLK * BLK), BF),
            pltpu.VMEM((max(unroll, -(-2 * half // (PITCH * BLK // 2 // LANES))), PITCH * BLK // 2, LANES), F32),
            pltpu.VMEM((half, 2 * LANES, 4 * LANES), BF),
            pltpu.VMEM((2,) + own_gram.shape, BF),
            pltpu.VMEM((blocks, BLK, LANES), BF),
            pltpu.VMEM((blocks, tall, channels * BLK), BF),
            pltpu.VMEM((blocks, 2 * rows, channels // 2 * BLK), BF),
            pltpu.VMEM((blocks, BLK, LANES), F32),
            pltpu.VMEM((blocks, 2 * rows, LANES), F32),
            pltpu.SemaphoreType.DMA((2,)),
        ],
        compiler_params=pltpu.CompilerParams(vmem_limit_bytes=48 << 20),
        cost_estimate=pl.CostEstimate(
            flops=6 * slots * channels * BLK * BLK * terms, bytes_accessed=observed.size * 2, transcendentals=0
        ),
    )(mine, other, own, got, observed, more, own_gram, got_gram)


def from_partner(array, mask):
    return lax.ppermute(array, "tile", [(i, i ^ mask) for i in range(lax.axis_size("tile"))])


def on_device(
    coefficients, zernike_table, positions, source_flux, observed, tile_rows, tile_cols, tile_count
):
    members = lax.axis_size("tile")
    terms, shard = coefficients.shape
    dishes = members * shard
    scale = 1.0 / math.sqrt(dishes * positions.shape[0])
    channels, slots = positions.shape[0], tile_rows.shape[0]
    moved = slots // 4 + 1
    mine = jnp.concatenate([tile_rows, tile_cols, tile_count])
    to_move = observed[slots - moved :]
    own_gram = gram_of(zernike_table, positions, source_flux)
    if shard == LANES and members == 16:
        held = coefficients[None]
        held = jnp.concatenate([held, from_partner(held, 8)], 0)
        held, own_gram = lax.optimization_barrier((held, own_gram))
        more, other = from_partner(to_move, 1), from_partner(mine, 1)
        got_gram = from_partner(own_gram, 1)
        held = jnp.concatenate([held] + [from_partner(held, mask) for mask in (6, 4, 2)][::-1], 0)
        held, got_gram, other = lax.optimization_barrier((held, got_gram, other))
        got = from_partner(held, 1)
        total, sent = tile_terms(
            True, scale, mine, other, held, got, own_gram, got_gram, observed, more
        )
        total = total + from_partner(sent, 1)
        total = sum(
            [from_partner(total[mask : mask + 2], mask) for mask in (6, 4, 2)], total[:2]
        )
        total = total[:1] + from_partner(total[1:], 8)
        return total[0]
    more, other, got_gram = (from_partner(array, 1) for array in (to_move, mine, own_gram))
    everything = lax.all_gather(coefficients, "tile", axis=1, tiled=True)
    everything = everything.reshape(terms, dishes // LANES, LANES).transpose(1, 0, 2)
    half = everything.shape[0] // 2
    parts = tile_terms(
        False, scale, mine, other, everything[:half], everything[half:], own_gram, got_gram, observed, more
    )
    total = jnp.concatenate(parts, 0).transpose(1, 0, 2).reshape(terms, dishes)
    return lax.psum_scatter(total, "tile", scatter_dimension=1, tiled=True)


def solution(mesh):
    return jax.shard_map(
        on_device,
        mesh=mesh,
        in_specs=(
            P(None, "tile"),
            P(),
            P("scan", None),
            P("scan", None),
            P(("scan", "tile"), None, None),
            P(("scan", "tile")),
            P(("scan", "tile")),
            P(("scan", "tile")),
        ),
        out_specs=P("scan", "tile"),
        check_vma=False,
    )
```

```python
import functools
import math

import jax
import jax.numpy as jnp
from jax import lax
from jax.experimental import pallas as pl
from jax.experimental.pallas import tpu as pltpu
from jax.sharding import PartitionSpec as P

BLK = 64
PITCH = 18
UNROLL = 7
LANES = 128
PIXELS = 256
BF = jnp.bfloat16
F32 = jnp.float32
NT = (((1,), (1,)), ((), ()))


def up(size, unit):
    return -(-size // unit) * unit


def sorting(size, transposed=False):
    natural = lax.broadcasted_iota(jnp.int32, (size, size), 1 if transposed else 0)
    place = lax.broadcasted_iota(jnp.int32, (size, size), 0 if transposed else 1)
    inside = place % BLK
    source = place - inside + inside % (BLK // 2) * 2 + inside // (BLK // 2)
    return jnp.where(natural == source, 1.0, 0.0).astype(BF)


def low_lanes(rows):
    return lax.broadcasted_iota(jnp.int32, (rows, LANES), 1) < BLK


def gram_kernel(root, table_ref, pos_ref, flux_ref, out_ref, groups, gram):
    terms, pixels = table_ref.shape
    channels, sources = pos_ref.shape
    count = channels // 2
    start = lax.axis_index("tile") % 2 * count
    n_groups = pixels // PIXELS
    tall = groups.shape[0] // n_groups
    rows = up(terms, 8)
    groups[...] = jnp.zeros_like(groups)
    gram[...] = jnp.zeros_like(gram)
    for h in range(n_groups):
        groups[h * tall : h * tall + terms, :] = table_ref[:, h * PIXELS : (h + 1) * PIXELS]
    pixel = lax.broadcasted_iota(jnp.int32, (PIXELS, sources), 0)
    for f in range(0, count, count):
        positions = [pos_ref[pl.ds(start + f + e, 1), :] for e in range(count)]
        hot = jnp.concatenate(
            [jnp.where(pixel == pos % PIXELS, 1.0, 0.0).astype(BF) for pos in positions], 1
        )
        found = jnp.dot(groups[...], hot, preferred_element_type=F32)
        for e, pos in enumerate(positions):
            group = pos // PIXELS
            chosen = jnp.zeros((tall, sources), F32)
            for h in range(n_groups):
                part = found[h * tall : (h + 1) * tall, e * sources : (e + 1) * sources]
                chosen = jnp.where(group == h, part, chosen)
            scaled = chosen * (flux_ref[pl.ds(start + f + e, 1), :] / root)
            high = scaled.astype(BF)
            low = (scaled - high.astype(F32)).astype(BF)
            chosen = chosen.astype(BF)
            product = lax.dot_general(high, chosen, NT, preferred_element_type=F32)
            product = product + lax.dot_general(low, chosen, NT, preferred_element_type=F32)
            gram[(f + e) * rows : (f + e) * rows + tall, 0:tall] = product
    value = gram[...]
    high = value.astype(BF)
    out_ref[:, 0:LANES] = high
    out_ref[:, LANES : 2 * LANES] = (value - high.astype(F32)).astype(BF)


def gram_of(zernike_table, positions, source_flux):
    terms, pixels = zernike_table.shape
    channels, sources = positions.shape
    count = channels // 2
    rows, tall = up(terms, 8), up(terms, 16)
    height = up(count * rows + 8, 16)
    return pl.pallas_call(
        functools.partial(gram_kernel, math.sqrt(sources)),
        out_shape=jax.ShapeDtypeStruct((height, 2 * LANES), BF),
        in_specs=[pl.BlockSpec(memory_space=pltpu.VMEM)] * 3,
        out_specs=pl.BlockSpec(memory_space=pltpu.VMEM),
        scratch_shapes=[
            pltpu.VMEM((pixels // PIXELS * tall, PIXELS), BF),
            pltpu.VMEM((height, LANES), F32),
        ],
        compiler_params=pltpu.CompilerParams(vmem_limit_bytes=32 << 20),
        cost_estimate=pl.CostEstimate(
            flops=2 * count * sources * pixels * terms, bytes_accessed=1 << 20, transcendentals=0
        ),
    )(zernike_table, positions, source_flux)


def relative_place(device, here):
    apart = device ^ here
    return 8 * (apart & 1) + (apart & 6) + (apart >> 3)


def tiles_kernel(
    relative, unroll, scale,
    mine_ref, other_ref, own_ref, got_ref, vis_hbm, more_hbm, own_gram_ref, got_gram_ref,
    keep_ref, send_ref,
    vis, stage, both, gram, turned, right, left, row_sum, col_sum, sems,
):
    slots, channels = vis.shape[0], vis.shape[1]
    kept = slots - more_hbm.shape[0]
    half, terms = own_ref.shape[0], own_ref.shape[1]
    pairs = channels // 2
    rows, tall = up(terms, 8), up(terms, 16)
    n_mine = jnp.minimum(mine_ref[2 * slots], kept)
    n_live = n_mine + jnp.maximum(other_ref[2 * slots] - kept, 0)
    copies = (
        pltpu.make_async_copy(vis_hbm.at[pl.ds(0, kept)], vis.at[pl.ds(0, kept)], sems.at[0]),
        pltpu.make_async_copy(more_hbm, vis.at[pl.ds(kept, slots - kept)], sems.at[1]),
    )
    for copy in copies:
        copy.start()

    row_sum[...] = jnp.zeros_like(row_sum)
    col_sum[...] = jnp.zeros_like(col_sum)
    both[...] = jnp.zeros_like(both)
    per_tile = stage.shape[1] // LANES

    for part, ref in enumerate((own_ref, got_ref)):
        for r in range(half):
            where = part * half + r
            chunk, lanes = where // 2, slice(where % 2 * LANES, (where % 2 + 1) * LANES)
            both[chunk, 0:terms, lanes] = ref[r]
            both[chunk, LANES : LANES + terms, lanes] = ref[r]
    order, order_of = sorting(2 * LANES), sorting(LANES, True)
    halves = jnp.concatenate([both[chunk, 0:LANES, 0 : 2 * LANES] for chunk in range(half)], 0)
    mixed = jnp.dot(halves, order, preferred_element_type=F32).astype(BF)
    for chunk in range(half):
        piece = mixed[chunk * LANES : (chunk + 1) * LANES]
        both[chunk, 0:LANES, 2 * LANES :] = piece
        both[chunk, LANES:, 2 * LANES :] = piece
    for chunk in range(half):
        for side in range(2):
            block = both[chunk, 0:LANES, side * LANES : (side + 1) * LANES]
            sorted_rows = lax.dot_general(order_of, block, NT, preferred_element_type=F32).astype(BF)
            turned[4 * chunk + 2 * side] = sorted_rows[0:BLK]
            turned[4 * chunk + 2 * side + 1] = sorted_rows[BLK:]

    here = lax.axis_index("tile")
    gram[here % 2] = own_gram_ref[...]
    gram[1 - here % 2] = got_gram_ref[...]
    low_r = low_lanes(tall)
    low_l = low_lanes(2 * rows)

    @pl.loop(0, half, unroll=8)
    def _(chunk):
        weights = both[chunk]
        for p in range(0, pairs, 2):
            start = p % (pairs // 2) * 2 * rows
            found = jnp.dot(
                gram[p // (pairs // 2), start : start + 4 * rows + 16, :],
                weights,
                preferred_element_type=F32,
            )
            for side in range(2):
                block = 4 * chunk + 2 * side
                part = found[:, side * LANES : (side + 1) * LANES]
                for e in range(2):
                    first = part[2 * e * rows : 2 * e * rows + tall]
                    second = part[(2 * e + 1) * rows : (2 * e + 1) * rows + tall]
                    lanes = slice((p + e) * LANES, (p + e + 1) * LANES)
                    first, second = first.astype(BF), second.astype(BF)
                    right[block, :, lanes] = jnp.concatenate([first[:, :BLK], second[:, :BLK]], 1)
                    right[block + 1, :, lanes] = jnp.concatenate([first[:, BLK:], second[:, BLK:]], 1)
                part = found[:, (side + 2) * LANES : (side + 3) * LANES]
                first, second = part[0 : 2 * rows], part[2 * rows : 4 * rows]
                lanes = slice(p * BLK, p * BLK + LANES)
                first, second = first.astype(BF), second.astype(BF)
                left[block, :, lanes] = jnp.concatenate([first[:, :BLK], second[:, :BLK]], 1)
                left[block + 1, :, lanes] = jnp.concatenate([first[:, BLK:], second[:, BLK:]], 1)

    row_pos = lax.broadcasted_iota(jnp.int32, (BLK, LANES), 0)
    row_dish = row_pos % (BLK // 2) * 2 + row_pos // (BLK // 2)
    ahead = lax.broadcasted_iota(jnp.int32, (BLK, LANES), 1) % BLK - row_dish
    low = low_lanes(BLK // 2)

    def place(block):
        return 2 * relative_place(block >> 1, here) + (block & 1) if relative else block

    for copy in copies:
        copy.wait()

    @pl.loop(0, (n_live + unroll - 1) // unroll)
    def _(group):
        slot_ids, pairs_of, leasts = [], [], []
        for u in range(unroll):
            turn = group * unroll + u
            is_mine = turn < n_mine
            slot = jnp.minimum(jnp.where(is_mine, turn, kept + turn - n_mine), slots - 1)
            row = jnp.where(is_mine, mine_ref[slot], other_ref[slot])
            col = jnp.where(is_mine, mine_ref[slots + slot], other_ref[slots + slot])
            slot_ids.append(slot)
            pairs_of.append((place(row), place(col)))
            leasts.append(jnp.where(turn < n_live, jnp.where(row == col, 0, -BLK), BLK))
        for u, slot in enumerate(slot_ids):
            for c in range(BLK // 2):
                stage[u, c * PITCH : c * PITCH + channels, :] = vis[
                    slot, :, c * LANES : (c + 1) * LANES
                ].astype(F32)
        models = [
            jnp.dot(turned[a][:, 0:tall], right[b], preferred_element_type=F32) for a, b in pairs_of
        ]
        residuals = []
        for u, slot in enumerate(slot_ids):
            keep = ahead > leasts[u]
            residual = []
            for p in range(pairs):
                first = stage[u, pl.ds(2 * p, BLK // 2, stride=PITCH), :]
                second = stage[u, pl.ds(2 * p + 1, BLK // 2, stride=PITCH), :]
                first, second = first.astype(BF), second.astype(BF)
                seen = jnp.concatenate(
                    [
                        jnp.concatenate([first[:, :BLK], second[:, :BLK]], 1),
                        jnp.concatenate([first[:, BLK:], second[:, BLK:]], 1),
                    ],
                    0,
                ).astype(F32)
                difference = models[u][:, p * LANES : (p + 1) * LANES] - seen
                residual.append(jnp.where(keep, difference, 0.0).astype(BF))
            residuals.append(residual)
        to_rows = [
            lax.dot_general(jnp.concatenate(residual, 1), right[b], NT, preferred_element_type=F32)
            for (a, b), residual in zip(pairs_of, residuals)
        ]
        to_cols = [
            jnp.dot(left[a], jnp.concatenate(residual, 0), preferred_element_type=F32)
            for (a, b), residual in zip(pairs_of, residuals)
        ]
        for (a, b), to_row, to_col in zip(pairs_of, to_rows, to_cols):
            row_sum[a, :, 0:tall] += to_row
            col_sum[b] += to_col

    low_out = low_lanes(rows)
    for where in range(2 * half):
        buf, base = where // per_tile, where % per_tile * LANES
        for side in range(2):
            total = row_sum[2 * where + side]
            start = base + side * BLK
            stage[buf, pl.ds(start, BLK // 2, stride=2), :] = total[0 : BLK // 2]
            stage[buf, pl.ds(start + 1, BLK // 2, stride=2), :] = total[BLK // 2 :]
    for where in range(2 * half):
        buf, base = where // per_tile, where % per_tile * LANES
        from_rows = stage[buf, base : base + LANES, :].T[0:rows]
        first, second = col_sum[2 * where], col_sum[2 * where + 1]
        straight = jnp.where(low_out, first[0:rows], second[rows:])
        crossed = jnp.where(low_out, second[0:rows], first[rows:])
        from_cols = straight + pltpu.roll(crossed, BLK, 1)
        result = ((from_rows + from_cols) * scale)[0:terms]
        if where < half:
            keep_ref[where] = result
        else:
            send_ref[where - half] = result


def tile_terms(relative, scale, mine, other, own, got, own_gram, got_gram, observed, more):
    slots, channels, _ = observed.shape
    half, terms, _ = own.shape
    rows, tall = up(terms, 8), up(terms, 16)
    blocks = 4 * half
    unroll = UNROLL
    smem = pl.BlockSpec(memory_space=pltpu.SMEM)
    vmem = pl.BlockSpec(memory_space=pltpu.VMEM)
    out = jax.ShapeDtypeStruct((half, terms, LANES), F32)
    return pl.pallas_call(
        functools.partial(tiles_kernel, relative, unroll, scale),
        out_shape=(out, out),
        in_specs=[smem, smem, vmem, vmem] + [pl.BlockSpec(memory_space=pl.ANY)] * 2 + [vmem] * 2,
        out_specs=(vmem, vmem),
        scratch_shapes=[
            pltpu.VMEM((slots, channels, BLK * BLK), BF),
            pltpu.VMEM((max(unroll, -(-2 * half // (PITCH * BLK // 2 // LANES))), PITCH * BLK // 2, LANES), F32),
            pltpu.VMEM((half, 2 * LANES, 4 * LANES), BF),
            pltpu.VMEM((2,) + own_gram.shape, BF),
            pltpu.VMEM((blocks, BLK, LANES), BF),
            pltpu.VMEM((blocks, tall, channels * BLK), BF),
            pltpu.VMEM((blocks, 2 * rows, channels // 2 * BLK), BF),
            pltpu.VMEM((blocks, BLK, LANES), F32),
            pltpu.VMEM((blocks, 2 * rows, LANES), F32),
            pltpu.SemaphoreType.DMA((2,)),
        ],
        compiler_params=pltpu.CompilerParams(vmem_limit_bytes=48 << 20),
        cost_estimate=pl.CostEstimate(
            flops=6 * slots * channels * BLK * BLK * terms, bytes_accessed=observed.size * 2, transcendentals=0
        ),
    )(mine, other, own, got, observed, more, own_gram, got_gram)


def from_partner(array, mask):
    return lax.ppermute(array, "tile", [(i, i ^ mask) for i in range(lax.axis_size("tile"))])


def on_device(
    coefficients, zernike_table, positions, source_flux, observed, tile_rows, tile_cols, tile_count
):
    members = lax.axis_size("tile")
    terms, shard = coefficients.shape
    dishes = members * shard
    scale = 1.0 / math.sqrt(dishes * positions.shape[0])
    channels, slots = positions.shape[0], tile_rows.shape[0]
    moved = slots // 4 + 1
    mine = jnp.concatenate([tile_rows, tile_cols, tile_count])
    to_move = observed[slots - moved :]
    own_gram = gram_of(zernike_table, positions, source_flux)
    if shard == LANES and members == 16:
        held = coefficients[None]
        held = jnp.concatenate([held, from_partner(held, 8)], 0)
        held, own_gram = lax.optimization_barrier((held, own_gram))
        more, other = from_partner(to_move, 1), from_partner(mine, 1)
        got_gram = from_partner(own_gram, 1)
        held = jnp.concatenate([held] + [from_partner(held, mask) for mask in (6, 4, 2)][::-1], 0)
        held, got_gram, other = lax.optimization_barrier((held, got_gram, other))
        got = from_partner(held, 1)
        total, sent = tile_terms(
            True, scale, mine, other, held, got, own_gram, got_gram, observed, more
        )
        total = total + from_partner(sent, 1)
        total = sum(
            [from_partner(total[mask : mask + 2].astype(BF), mask).astype(F32) for mask in (6, 4, 2)],
            total[:2],
        )
        total = total[:1] + from_partner(total[1:], 8)
        return total[0]
    more, other, got_gram = (from_partner(array, 1) for array in (to_move, mine, own_gram))
    everything = lax.all_gather(coefficients, "tile", axis=1, tiled=True)
    everything = everything.reshape(terms, dishes // LANES, LANES).transpose(1, 0, 2)
    half = everything.shape[0] // 2
    parts = tile_terms(
        False, scale, mine, other, everything[:half], everything[half:], own_gram, got_gram, observed, more
    )
    total = jnp.concatenate(parts, 0).transpose(1, 0, 2).reshape(terms, dishes)
    return lax.psum_scatter(total, "tile", scatter_dimension=1, tiled=True)


def solution(mesh):
    return jax.shard_map(
        on_device,
        mesh=mesh,
        in_specs=(
            P(None, "tile"),
            P(),
            P("scan", None),
            P("scan", None),
            P(("scan", "tile"), None, None),
            P(("scan", "tile")),
            P(("scan", "tile")),
            P(("scan", "tile")),
        ),
        out_specs=P("scan", "tile"),
        check_vma=False,
    )
```

```python
import functools
import math

import jax
import jax.numpy as jnp
from jax import lax
from jax.experimental import pallas as pl
from jax.experimental.pallas import tpu as pltpu
from jax.sharding import PartitionSpec as P

BLK = 64
PITCH = 18
UNROLL = 7
LANES = 128
PIXELS = 256
BF = jnp.bfloat16
F32 = jnp.float32
NT = (((1,), (1,)), ((), ()))


def up(size, unit):
    return -(-size // unit) * unit


def sorting(size, transposed=False):
    natural = lax.broadcasted_iota(jnp.int32, (size, size), 1 if transposed else 0)
    place = lax.broadcasted_iota(jnp.int32, (size, size), 0 if transposed else 1)
    inside = place % BLK
    source = place - inside + inside % (BLK // 2) * 2 + inside // (BLK // 2)
    return jnp.where(natural == source, 1.0, 0.0).astype(BF)


def low_lanes(rows):
    return lax.broadcasted_iota(jnp.int32, (rows, LANES), 1) < BLK


def gram_kernel(root, table_ref, pos_ref, flux_ref, out_ref, groups, gram):
    terms, pixels = table_ref.shape
    channels, sources = pos_ref.shape
    count = channels // 2
    start = lax.axis_index("tile") % 2 * count
    n_groups = pixels // PIXELS
    tall = groups.shape[0] // n_groups
    rows = up(terms, 8)
    groups[...] = jnp.zeros_like(groups)
    gram[...] = jnp.zeros_like(gram)
    for h in range(n_groups):
        groups[h * tall : h * tall + terms, :] = table_ref[:, h * PIXELS : (h + 1) * PIXELS]
    pixel = lax.broadcasted_iota(jnp.int32, (PIXELS, sources), 0)
    for f in range(0, count, count):
        positions = [pos_ref[pl.ds(start + f + e, 1), :] for e in range(count)]
        hot = jnp.concatenate(
            [jnp.where(pixel == pos % PIXELS, 1.0, 0.0).astype(BF) for pos in positions], 1
        )
        found = jnp.dot(groups[...], hot, preferred_element_type=F32)
        for e, pos in enumerate(positions):
            group = pos // PIXELS
            chosen = jnp.zeros((tall, sources), F32)
            for h in range(n_groups):
                part = found[h * tall : (h + 1) * tall, e * sources : (e + 1) * sources]
                chosen = jnp.where(group == h, part, chosen)
            scaled = chosen * (flux_ref[pl.ds(start + f + e, 1), :] / root)
            high = scaled.astype(BF)
            low = (scaled - high.astype(F32)).astype(BF)
            chosen = chosen.astype(BF)
            product = lax.dot_general(high, chosen, NT, preferred_element_type=F32)
            product = product + lax.dot_general(low, chosen, NT, preferred_element_type=F32)
            gram[(f + e) * rows : (f + e) * rows + tall, 0:tall] = product
    value = gram[...]
    high = value.astype(BF)
    out_ref[:, 0:LANES] = high
    out_ref[:, LANES : 2 * LANES] = (value - high.astype(F32)).astype(BF)


def gram_of(zernike_table, positions, source_flux):
    terms, pixels = zernike_table.shape
    channels, sources = positions.shape
    count = channels // 2
    rows, tall = up(terms, 8), up(terms, 16)
    height = up(count * rows + 8, 16)
    return pl.pallas_call(
        functools.partial(gram_kernel, math.sqrt(sources)),
        out_shape=jax.ShapeDtypeStruct((height, 2 * LANES), BF),
        in_specs=[pl.BlockSpec(memory_space=pltpu.VMEM)] * 3,
        out_specs=pl.BlockSpec(memory_space=pltpu.VMEM),
        scratch_shapes=[
            pltpu.VMEM((pixels // PIXELS * tall, PIXELS), BF),
            pltpu.VMEM((height, LANES), F32),
        ],
        compiler_params=pltpu.CompilerParams(vmem_limit_bytes=32 << 20),
        cost_estimate=pl.CostEstimate(
            flops=2 * count * sources * pixels * terms, bytes_accessed=1 << 20, transcendentals=0
        ),
    )(zernike_table, positions, source_flux)


def relative_place(device, here):
    apart = device ^ here
    return 8 * (apart & 1) + (apart & 6) + (apart >> 3)


def tiles_kernel(
    relative, unroll, scale,
    mine_ref, other_ref, own_ref, got_ref, vis_hbm, more_hbm, own_gram_ref, got_gram_ref,
    keep_ref, send_ref,
    vis, stage, both, gram, turned, right, left, row_sum, col_sum, sems,
):
    slots, channels = vis.shape[0], vis.shape[1]
    kept = slots - more_hbm.shape[0]
    half, terms = own_ref.shape[0], own_ref.shape[1]
    pairs = channels // 2
    rows, tall = up(terms, 8), up(terms, 16)
    n_mine = jnp.minimum(mine_ref[2 * slots], kept)
    n_live = n_mine + jnp.maximum(other_ref[2 * slots] - kept, 0)
    copies = (
        pltpu.make_async_copy(vis_hbm.at[pl.ds(0, kept)], vis.at[pl.ds(0, kept)], sems.at[0]),
        pltpu.make_async_copy(more_hbm, vis.at[pl.ds(kept, slots - kept)], sems.at[1]),
    )
    for copy in copies:
        copy.start()

    row_sum[...] = jnp.zeros_like(row_sum)
    col_sum[...] = jnp.zeros_like(col_sum)
    both[...] = jnp.zeros_like(both)
    per_tile = stage.shape[1] // LANES

    for part, ref in enumerate((own_ref, got_ref)):
        for r in range(half):
            where = part * half + r
            chunk, lanes = where // 2, slice(where % 2 * LANES, (where % 2 + 1) * LANES)
            both[chunk, 0:terms, lanes] = ref[r]
            both[chunk, LANES : LANES + terms, lanes] = ref[r]
    order, order_of = sorting(2 * LANES), sorting(LANES, True)
    halves = jnp.concatenate([both[chunk, 0:LANES, 0 : 2 * LANES] for chunk in range(half)], 0)
    mixed = jnp.dot(halves, order, preferred_element_type=F32).astype(BF)
    for chunk in range(half):
        piece = mixed[chunk * LANES : (chunk + 1) * LANES]
        both[chunk, 0:LANES, 2 * LANES :] = piece
        both[chunk, LANES:, 2 * LANES :] = piece
    for chunk in range(half):
        for side in range(2):
            block = both[chunk, 0:LANES, side * LANES : (side + 1) * LANES]
            sorted_rows = lax.dot_general(order_of, block, NT, preferred_element_type=F32).astype(BF)
            turned[4 * chunk + 2 * side] = sorted_rows[0:BLK]
            turned[4 * chunk + 2 * side + 1] = sorted_rows[BLK:]

    here = lax.axis_index("tile")
    gram[here % 2] = own_gram_ref[...]
    gram[1 - here % 2] = got_gram_ref[...]
    low_r = low_lanes(tall)
    low_l = low_lanes(2 * rows)

    @pl.loop(0, half, unroll=8)
    def _(chunk):
        weights = both[chunk]
        for p in range(0, pairs, 2):
            start = p % (pairs // 2) * 2 * rows
            found = jnp.dot(
                gram[p // (pairs // 2), start : start + 4 * rows + 16, :],
                weights,
                preferred_element_type=F32,
            )
            for side in range(2):
                block = 4 * chunk + 2 * side
                part = found[:, side * LANES : (side + 1) * LANES]
                for e in range(2):
                    first = part[2 * e * rows : 2 * e * rows + tall]
                    second = part[(2 * e + 1) * rows : (2 * e + 1) * rows + tall]
                    lanes = slice((p + e) * LANES, (p + e + 1) * LANES)
                    first, second = first.astype(BF), second.astype(BF)
                    right[block, :, lanes] = jnp.concatenate([first[:, :BLK], second[:, :BLK]], 1)
                    right[block + 1, :, lanes] = jnp.concatenate([first[:, BLK:], second[:, BLK:]], 1)
                part = found[:, (side + 2) * LANES : (side + 3) * LANES]
                first, second = part[0 : 2 * rows], part[2 * rows : 4 * rows]
                lanes = slice(p * BLK, p * BLK + LANES)
                first, second = first.astype(BF), second.astype(BF)
                left[block, :, lanes] = jnp.concatenate([first[:, :BLK], second[:, :BLK]], 1)
                left[block + 1, :, lanes] = jnp.concatenate([first[:, BLK:], second[:, BLK:]], 1)

    row_pos = lax.broadcasted_iota(jnp.int32, (BLK, LANES), 0)
    row_dish = row_pos % (BLK // 2) * 2 + row_pos // (BLK // 2)
    ahead = lax.broadcasted_iota(jnp.int32, (BLK, LANES), 1) % BLK - row_dish
    low = low_lanes(BLK // 2)

    def place(block):
        return 2 * relative_place(block >> 1, here) + (block & 1) if relative else block

    for copy in copies:
        copy.wait()

    @pl.loop(0, (n_live + unroll - 1) // unroll)
    def _(group):
        slot_ids, pairs_of, leasts = [], [], []
        for u in range(unroll):
            turn = group * unroll + u
            is_mine = turn < n_mine
            slot = jnp.minimum(jnp.where(is_mine, turn, kept + turn - n_mine), slots - 1)
            row = jnp.where(is_mine, mine_ref[slot], other_ref[slot])
            col = jnp.where(is_mine, mine_ref[slots + slot], other_ref[slots + slot])
            slot_ids.append(slot)
            pairs_of.append((place(row), place(col)))
            leasts.append(jnp.where(turn < n_live, jnp.where(row == col, 0, -BLK), BLK))
        for u, slot in enumerate(slot_ids):
            for c in range(BLK // 2):
                stage[u, c * PITCH : c * PITCH + channels, :] = vis[
                    slot, :, c * LANES : (c + 1) * LANES
                ].astype(F32)
        models = [
            jnp.dot(turned[a][:, 0:tall], right[b], preferred_element_type=F32) for a, b in pairs_of
        ]
        residuals = []
        for u, slot in enumerate(slot_ids):
            keep = ahead > leasts[u]
            residual = []
            for p in range(pairs):
                first = stage[u, pl.ds(2 * p, BLK // 2, stride=PITCH), :]
                second = stage[u, pl.ds(2 * p + 1, BLK // 2, stride=PITCH), :]
                first, second = first.astype(BF), second.astype(BF)
                seen = jnp.concatenate(
                    [
                        jnp.concatenate([first[:, :BLK], second[:, :BLK]], 1),
                        jnp.concatenate([first[:, BLK:], second[:, BLK:]], 1),
                    ],
                    0,
                ).astype(F32)
                difference = models[u][:, p * LANES : (p + 1) * LANES] - seen
                residual.append(jnp.where(keep, difference, 0.0).astype(BF))
            residuals.append(residual)
        to_rows, to_cols = [], []
        for (a, b), residual in zip(pairs_of, residuals):
            to_cols.append(jnp.dot(left[a], jnp.concatenate(residual, 0), preferred_element_type=F32))
            to_rows.append(
                lax.dot_general(jnp.concatenate(residual, 1), right[b], NT, preferred_element_type=F32)
            )
        for (a, b), to_row, to_col in zip(pairs_of, to_rows, to_cols):
            row_sum[a, :, 0:tall] += to_row
            col_sum[b] += to_col

    low_out = low_lanes(rows)
    for where in range(2 * half):
        buf, base = where // per_tile, where % per_tile * LANES
        for side in range(2):
            total = row_sum[2 * where + side]
            start = base + side * BLK
            stage[buf, pl.ds(start, BLK // 2, stride=2), :] = total[0 : BLK // 2]
            stage[buf, pl.ds(start + 1, BLK // 2, stride=2), :] = total[BLK // 2 :]
    for where in range(2 * half):
        buf, base = where // per_tile, where % per_tile * LANES
        from_rows = stage[buf, base : base + LANES, :].T[0:rows]
        first, second = col_sum[2 * where], col_sum[2 * where + 1]
        straight = jnp.where(low_out, first[0:rows], second[rows:])
        crossed = jnp.where(low_out, second[0:rows], first[rows:])
        from_cols = straight + pltpu.roll(crossed, BLK, 1)
        result = ((from_rows + from_cols) * scale)[0:terms]
        if where < half:
            keep_ref[where] = result
        else:
            send_ref[where - half] = result


def tile_terms(relative, scale, mine, other, own, got, own_gram, got_gram, observed, more):
    slots, channels, _ = observed.shape
    half, terms, _ = own.shape
    rows, tall = up(terms, 8), up(terms, 16)
    blocks = 4 * half
    staged = up(PITCH * (BLK // 2 + 1), 8)
    unroll = UNROLL
    smem = pl.BlockSpec(memory_space=pltpu.SMEM)
    vmem = pl.BlockSpec(memory_space=pltpu.VMEM)
    out = jax.ShapeDtypeStruct((half, terms, LANES), F32)
    return pl.pallas_call(
        functools.partial(tiles_kernel, relative, unroll, scale),
        out_shape=(out, out),
        in_specs=[smem, smem, vmem, vmem] + [pl.BlockSpec(memory_space=pl.ANY)] * 2 + [vmem] * 2,
        out_specs=(vmem, vmem),
        scratch_shapes=[
            pltpu.VMEM((slots, channels, BLK * BLK), BF),
            pltpu.VMEM((max(unroll, -(-2 * half // (staged // LANES))), staged, LANES), F32),
            pltpu.VMEM((half, 2 * LANES, 4 * LANES), BF),
            pltpu.VMEM((2,) + own_gram.shape, BF),
            pltpu.VMEM((blocks, BLK, LANES), BF),
            pltpu.VMEM((blocks, tall, channels * BLK), BF),
            pltpu.VMEM((blocks, 2 * rows, channels // 2 * BLK), BF),
            pltpu.VMEM((blocks, BLK, LANES), F32),
            pltpu.VMEM((blocks, 2 * rows, LANES), F32),
            pltpu.SemaphoreType.DMA((2,)),
        ],
        compiler_params=pltpu.CompilerParams(vmem_limit_bytes=48 << 20),
        cost_estimate=pl.CostEstimate(
            flops=6 * slots * channels * BLK * BLK * terms, bytes_accessed=observed.size * 2, transcendentals=0
        ),
    )(mine, other, own, got, observed, more, own_gram, got_gram)


def from_partner(array, mask):
    return lax.ppermute(array, "tile", [(i, i ^ mask) for i in range(lax.axis_size("tile"))])


def on_device(
    coefficients, zernike_table, positions, source_flux, observed, tile_rows, tile_cols, tile_count
):
    members = lax.axis_size("tile")
    terms, shard = coefficients.shape
    dishes = members * shard
    scale = 1.0 / math.sqrt(dishes * positions.shape[0])
    channels, slots = positions.shape[0], tile_rows.shape[0]
    moved = slots // 4 + 1
    mine = jnp.concatenate([tile_rows, tile_cols, tile_count])
    to_move = observed[slots - moved :]
    own_gram = gram_of(zernike_table, positions, source_flux)
    if shard == LANES and members == 16:
        held = coefficients[None]
        held = jnp.concatenate([held, from_partner(held, 8)], 0)
        held, own_gram = lax.optimization_barrier((held, own_gram))
        more, other = from_partner(to_move, 1), from_partner(mine, 1)
        got_gram = from_partner(own_gram, 1)
        held = jnp.concatenate([held] + [from_partner(held, mask) for mask in (6, 4, 2)][::-1], 0)
        held, got_gram, other = lax.optimization_barrier((held, got_gram, other))
        got = from_partner(held, 1)
        total, sent = tile_terms(
            True, scale, mine, other, held, got, own_gram, got_gram, observed, more
        )
        total = total + from_partner(sent, 1)
        total = sum(
            [from_partner(total[mask : mask + 2].astype(BF), mask).astype(F32) for mask in (6, 4, 2)],
            total[:2],
        )
        total = total[:1] + from_partner(total[1:], 8)
        return total[0]
    more, other, got_gram = (from_partner(array, 1) for array in (to_move, mine, own_gram))
    everything = lax.all_gather(coefficients, "tile", axis=1, tiled=True)
    everything = everything.reshape(terms, dishes // LANES, LANES).transpose(1, 0, 2)
    half = everything.shape[0] // 2
    parts = tile_terms(
        False, scale, mine, other, everything[:half], everything[half:], own_gram, got_gram, observed, more
    )
    total = jnp.concatenate(parts, 0).transpose(1, 0, 2).reshape(terms, dishes)
    return lax.psum_scatter(total, "tile", scatter_dimension=1, tiled=True)


def solution(mesh):
    return jax.shard_map(
        on_device,
        mesh=mesh,
        in_specs=(
            P(None, "tile"),
            P(),
            P("scan", None),
            P("scan", None),
            P(("scan", "tile"), None, None),
            P(("scan", "tile")),
            P(("scan", "tile")),
            P(("scan", "tile")),
        ),
        out_specs=P("scan", "tile"),
        check_vma=False,
    )
```
